256 devices in a mesh: seq: 32 (over z, x), head: 8 (over y, core).
Axes of the slice: x: 4, y: 4, z: 8, core: 2. Of those that a mesh axis runs over, the one named last changes fastest.
Arguments:
- queries: bfloat16 [32768, 4096], P('seq', 'head'), may hold values from -4 to 4
- keys: bfloat16 [32768, 4096], P('seq', 'head'), may hold values from -4 to 4
- values: bfloat16 [32768, 4096], P('seq', 'head'), may hold values from -100 to 100
- gain: float32 [4096], P('head'), may hold values from 0.5 to 1.5
- grad_out: bfloat16 [32768, 4096], P('seq', 'head'), may hold values from -100 to 100
Outputs:
- normed: bfloat16 [32768, 4096], P('seq', 'head')
- grad_queries: bfloat16 [32768, 4096], P('seq', 'head')
- grad_keys: bfloat16 [32768, 4096], P('seq', 'head')
- grad_values: bfloat16 [32768, 4096], P('seq', 'head')
The draws below stay inside these ranges and needn't reach their ends.
All inputs are finite; a program needn't handle non-finite values.
Results may differ from the reference program's by a relative error of at most 0.0058.
Values sent between devices are 32-bit elements; how exact they have to be, the bound alone decides.
A program may use at most 128 MiB of HBM per device.

```python
import math
import jax
import jax.numpy as jnp
from jax import lax

HEADS = 32
HD = 128
D = 4096
BLK = 512
TOKENS = 32768


def rough_field(key, rise, spread, divisor):
    parts = jax.random.split(key, 3)
    base = jnp.clip(jax.random.normal(parts[0], (TOKENS, D), jnp.float32), -4.0, 4.0)
    row_scale = jnp.exp(jax.random.uniform(parts[1], (TOKENS, 1), jnp.float32) * math.log(spread))
    col_scale = jnp.exp(jax.random.uniform(parts[2], (1, D), jnp.float32) * math.log(10.0))
    heads = (jnp.arange(D) // HD).astype(jnp.float32)
    head_scale = rise ** (heads / (HEADS - 1))
    return base * row_scale * col_scale * head_scale / divisor


def draw_values(key, part):
    key = jax.random.fold_in(key, 11)
    field = rough_field(key, 1.7320508, 10.0, 10.0)
    return field.astype(jnp.bfloat16)


def draw_grad_out(key, part):
    key = jax.random.fold_in(key, 23)
    field = rough_field(key, 1.7320508, 10.0, 10.0)
    return field.astype(jnp.bfloat16)


def level_of(key, shape, cuts, least, largest):
    def one(position, blocks):
        steps = jax.random.uniform(jax.random.fold_in(jax.random.fold_in(key, 6), position), (blocks,), jnp.float32, least / len(cuts), largest / len(cuts))
        return jnp.repeat(jnp.exp(steps), shape[position] // blocks).reshape((-1,) + (1,) * (len(shape) - position - 1))

    factor_of = one(*cuts[0])
    for cut in cuts[1:]:
        factor_of = factor_of * one(*cut)
    return factor_of


def centred(stream_key, shape, scale, most, shards=(), kind=jnp.bfloat16):
    array = scale * jax.random.normal(stream_key, shape, jnp.float32)
    if shards:
        array = array * level_of(stream_key, shape, shards, -0.22, 0.18)
    return jnp.clip(array, -most, most).astype(kind)


def setup_inputs(seed: int = 0) -> dict:
    key_of = jax.random.split(jax.random.key(seed), 6)
    return {
        "queries": centred(key_of[0], (TOKENS, D), 1.0, 4.0, ((0, 32), (1, 8))),
        "keys": centred(key_of[1], (TOKENS, D), 1.0, 4.0, ((0, 32), (1, 8))),
        "values": draw_values(jax.random.fold_in(key_of[5], 71), 0),
        "gain": jnp.clip(1.0 + 0.1 * jax.random.normal(key_of[3], (D,), jnp.float32), 0.5, 1.5),
        "grad_out": draw_grad_out(jax.random.fold_in(key_of[5], 71), 0),
    }


EPS = 1e-06

def reference(queries, keys, values, gain, grad_out):
    nb = TOKENS // BLK
    f32 = jnp.float32
    bf16 = jnp.bfloat16
    qs = queries.reshape(nb, BLK, HEADS, HD)
    ks = keys.reshape(nb, BLK, HEADS, HD)
    vs = values.reshape(nb, BLK, HEADS, HD)
    mask = jnp.arange(BLK)[None, :] <= jnp.arange(BLK)[:, None]

    def forward(state, xs):
        qb, kb, vb = [x.astype(f32) for x in xs]
        scores = jnp.einsum('shd,thd->hst', qb, kb)
        a_bf = jnp.where(mask, scores, 0.0).astype(bf16)
        state_bf = state.astype(bf16)
        num = jnp.einsum('hst,the->she', a_bf.astype(f32), vb) + jnp.einsum('shd,hde->she', qb, state_bf.astype(f32))
        state = state + jnp.einsum('thd,the->hde', kb, vb)
        return (state, (num, state_bf))
    _, (num, states) = lax.scan(forward, jnp.zeros((HEADS, HD, HD), f32), (qs, ks, vs))
    gains = gain.reshape(HEADS, HD)
    ratio = lax.rsqrt(lax.optimization_barrier(jnp.sum(num * num, axis=(2, 3))) / D + EPS)[:, :, None, None]
    normed = (num * ratio * gains).astype(bf16).reshape(TOKENS, D)
    scaled = grad_out.astype(f32).reshape(nb, BLK, HEADS, HD) * gains
    inner = (lax.optimization_barrier(jnp.sum(scaled * num, axis=(2, 3))) / D)[:, :, None, None]
    dnum = (ratio * (scaled - ratio * ratio * inner * num)).astype(bf16)

    def backward(later, xs):
        qb, kb, vb, db = [x.astype(f32) for x in xs[:4]]
        state_f = xs[4].astype(f32)
        scores = jnp.einsum('shd,thd->hst', qb, kb)
        a_f = jnp.where(mask, scores, 0.0).astype(bf16).astype(f32)
        later_f = later.astype(bf16).astype(f32)
        bmat = jnp.where(mask, jnp.einsum('she,the->hst', db, vb), 0.0).astype(bf16).astype(f32)
        grad_q = jnp.einsum('hst,thd->shd', bmat, kb) + jnp.einsum('she,hde->shd', db, state_f)
        grad_k = jnp.einsum('hst,shd->thd', bmat, qb) + jnp.einsum('the,hde->thd', vb, later_f)
        grad_v = jnp.einsum('hst,she->the', a_f, db) + jnp.einsum('thd,hde->the', kb, later_f)
        later = later + jnp.einsum('shd,she->hde', qb, db)
        return (later, (grad_q.astype(bf16), grad_k.astype(bf16), grad_v.astype(bf16)))
    _, (grad_q, grad_k, grad_v) = lax.scan(backward, jnp.zeros((HEADS, HD, HD), f32), (qs, ks, vs, dnum, states), reverse=True)
    return (normed, grad_q.reshape(TOKENS, D), grad_k.reshape(TOKENS, D), grad_v.reshape(TOKENS, D))
```

```python
import functools

import jax
import jax.numpy as jnp
from jax import lax
from jax.experimental import pallas as pl
from jax.experimental.pallas import tpu as pltpu
from jax.sharding import PartitionSpec as P

HD = 128
BLK = 512
HALF = BLK // 2
EPS = 1e-06
SLICE = 8
MESH = pl.DeviceIdType.MESH

F32 = jnp.float32
BF16 = jnp.bfloat16

NN = (((1,), (0,)), ((), ()))
NT = (((1,), (1,)), ((), ()))
TN = (((0,), (0,)), ((), ()))


def dot(a, b, dims):
    return lax.dot_general(a, b, dims, preferred_element_type=F32)


def lower(rows, columns, offset):
    s = lax.broadcasted_iota(jnp.int32, (rows, columns), 0) + offset
    t = lax.broadcasted_iota(jnp.int32, (rows, columns), 1)
    return t <= s


def upper(rows, columns):
    t = lax.broadcasted_iota(jnp.int32, (rows, columns), 0)
    s = lax.broadcasted_iota(jnp.int32, (rows, columns), 1)
    return t <= s


def masked(scores, mask):
    return jnp.where(mask, scores, 0.0).astype(BF16)


def kernel(
    n_seq,
    n_head,
    width,
    q_hbm,
    k_hbm,
    v_hbm,
    gain_ref,
    g_hbm,
    normed_hbm,
    gq_hbm,
    gk_hbm,
    gv_hbm,
    q,
    k,
    v,
    g,
    num,
    dn,
    first,
    local,
    state,
    a_t,
    gk_part,
    gv_part,
    normed,
    gq,
    gk,
    gv,
    gathered,
    prefix,
    arrived,
    stats,
    all_stats,
    in_sem,
    out_sem,
    send_sem,
    recv_sem,
    stat_send,
    stat_recv,
):
    rows, columns = q.shape
    heads = columns // HD
    chunks = heads // 2
    blocks = rows // BLK
    seq = lax.axis_index("seq")
    head = lax.axis_index("head")
    seq_partners = [lax.rem(seq + d, n_seq) for d in range(1, n_seq)]
    head_partners = [lax.rem(head + d, n_head) for d in range(1, n_head)]

    def cols(c):
        return slice(c * 2 * HD, (c + 1) * 2 * HD)

    loads = {}
    for c in range(chunks):
        for i, (name, src, dst) in enumerate((("k", k_hbm, k), ("v", v_hbm, v))):
            loads[name, c] = pltpu.make_async_copy(
                src.at[:, cols(c)], dst.at[:, cols(c)], in_sem.at[2 * c + i]
            )
            loads[name, c].start()
    for i, (name, src, dst) in enumerate((("q", q_hbm, q), ("g", g_hbm, g))):
        loads[name] = pltpu.make_async_copy(src, dst, in_sem.at[2 * chunks + i])
        loads[name].start()

    barrier = pltpu.get_barrier_semaphore()
    for p in seq_partners:
        pl.semaphore_signal(barrier, inc=1, device_id=(p, head), device_id_type=MESH)
    for p in head_partners:
        pl.semaphore_signal(barrier, inc=1, device_id=(seq, p), device_id_type=MESH)

    def exchange(scan, phase, c, source, landing):
        at = ((scan * 2) + phase) * chunks + c
        for p in seq_partners:
            pltpu.make_async_remote_copy(
                src_ref=source(p),
                dst_ref=landing,
                send_sem=send_sem.at[at],
                recv_sem=recv_sem.at[at],
                device_id=(p, head),
                device_id_type=MESH,
            ).start()

    def wait_exchange(scan, phase, c):
        at = ((scan * 2) + phase) * chunks + c
        n = n_seq - 1
        pltpu.make_async_copy(
            gathered.at[scan, c, pl.ds(0, n)],
            gathered.at[scan, c, pl.ds(0, n)],
            recv_sem.at[at],
        ).wait()

    def wait_sent(scan, phase, c):
        at = ((scan * 2) + phase) * chunks + c
        n = n_seq - 1
        pltpu.make_async_copy(
            gathered.at[scan, c, pl.ds(0, n)],
            gathered.at[scan, c, pl.ds(0, n)],
            send_sem.at[at],
        ).wait()

    def scatter(scan, c):
        gathered[scan, c, seq] = local[scan, c, seq]
        exchange(
            scan, 0, c, lambda p: local.at[scan, c, p], gathered.at[scan, c, seq]
        )

    def scan_and_return(scan, c):
        wait_exchange(scan, 0, c)
        total = jnp.zeros((SLICE, HD), F32)
        order = range(n_seq) if scan == 0 else range(n_seq - 1, -1, -1)
        for j in order:
            prefix[scan, c, j] = total
            total = total + gathered[scan, c, j]
        arrived[scan, c, seq] = prefix[scan, c, seq]
        exchange(
            scan, 1, c, lambda p: prefix.at[scan, c, p], arrived.at[scan, c, seq]
        )

    def outer_products(scan, c, left, right, keep):
        for i in range(2):
            h = 2 * c + i
            lane = slice(h * HD, (h + 1) * HD)
            parts = [
                dot(left[b * BLK : (b + 1) * BLK, lane], right[b * BLK : (b + 1) * BLK, lane], TN)
                for b in range(blocks)
            ]
            first[scan, c, i] = parts[keep]
            per = HD // SLICE
            local[scan, c, i * per : (i + 1) * per] = (parts[0] + parts[1]).reshape(
                per, SLICE, HD
            )

    for c in range(chunks):
        loads["k", c].wait()
        loads["v", c].wait()
        outer_products(0, c, k, v, 0)
        if c == 0:
            pl.semaphore_wait(barrier, n_seq - 1 + n_head - 1)
        scatter(0, c)

    loads["q"].wait()

    def scores(i, _):
        h = i // blocks
        b = lax.rem(i, blocks)
        lane = pl.ds(pl.multiple_of(h * HD, HD), HD)
        r0 = pl.multiple_of(b * BLK, BLK)
        lo, hi, both = pl.ds(r0, HALF), pl.ds(r0 + HALF, HALF), pl.ds(r0, BLK)
        a0 = masked(dot(q[lo, lane], k[lo, lane], NT), lower(HALF, HALF, 0))
        a1 = masked(dot(q[hi, lane], k[both, lane], NT), lower(HALF, BLK, HALF))
        num[lo, lane] = dot(a0, v[lo, lane], NN)
        num[hi, lane] = dot(a1, v[both, lane], NN)
        t0 = masked(dot(k[lo, lane], q[both, lane], NT), upper(HALF, BLK))
        t1 = masked(dot(k[hi, lane], q[hi, lane], NT), upper(HALF, HALF))
        a_t[h, b, 0:HALF, :] = t0
        a_t[h, b, HALF:BLK, HALF:BLK] = t1
        return 0

    lax.fori_loop(0, heads * blocks, scores, 0)

    for c in range(chunks):
        scan_and_return(0, c)

    loads["g"].wait()
    square = [None] * blocks
    product = [None] * blocks
    for c in range(chunks):
        wait_exchange(0, 1, c)
        for i in range(2):
            h = 2 * c + i
            lane = slice(h * HD, (h + 1) * HD)
            per = HD // SLICE
            incoming = arrived[0, c, i * per : (i + 1) * per].reshape(HD, HD)
            for b in range(blocks):
                row = slice(b * BLK, (b + 1) * BLK)
                s_bf = (incoming if b == 0 else incoming + first[0, c, i]).astype(BF16)
                state[h, b] = s_bf
                n = num[row, lane] + dot(q[row, lane], s_bf, NN)
                num[row, lane] = n
                gn = g[row, lane].astype(F32) * gain_ref[:, lane]
                sq, pr = n * n, gn * n
                square[b] = sq if square[b] is None else square[b] + sq
                product[b] = pr if product[b] is None else product[b] + pr

    ones = jnp.ones((SLICE, HD), BF16)

    def across(x):
        hi = x.astype(BF16)
        rest = x - hi.astype(F32)
        mid = rest.astype(BF16)
        low = (rest - mid.astype(F32)).astype(BF16)
        return (dot(ones, hi, NT) + dot(ones, mid, NT) + dot(ones, low, NT))[0:1]

    for b in range(blocks):
        stats[b : b + 1, :] = across(square[b])
        stats[blocks + b : blocks + b + 1, :] = across(product[b])
    all_stats[head] = stats[...]
    for p in head_partners:
        pltpu.make_async_remote_copy(
            src_ref=stats,
            dst_ref=all_stats.at[head],
            send_sem=stat_send,
            recv_sem=stat_recv,
            device_id=(seq, p),
            device_id_type=MESH,
        ).start()

    def stat_wait(sem):
        view = all_stats.at[pl.ds(0, n_head - 1)]
        pltpu.make_async_copy(view, view, sem).wait()

    stat_wait(stat_recv)
    totals = all_stats[0]
    for j in range(1, n_head):
        totals = totals + all_stats[j]
    ratio = lax.rsqrt(totals[0:blocks] / width + EPS)
    inner = totals[blocks:] / width
    weight = ratio * ratio * inner
    packed = jnp.concatenate([ratio, weight, jnp.zeros((8 - 2 * blocks, BLK), F32)], axis=0)
    turned = jnp.transpose(packed)
    ratios = [jnp.broadcast_to(turned[:, b : b + 1], (BLK, HD)) for b in range(blocks)]
    weights = [
        jnp.broadcast_to(turned[:, blocks + b : blocks + b + 1], (BLK, HD))
        for b in range(blocks)
    ]

    for c in range(chunks):
        for i in range(2):
            lane = slice((2 * c + i) * HD, (2 * c + i + 1) * HD)
            for b in range(blocks):
                row = slice(b * BLK, (b + 1) * BLK)
                n = num[row, lane]
                gn = g[row, lane].astype(F32) * gain_ref[:, lane]
                dn[row, lane] = (ratios[b] * (gn - weights[b] * n)).astype(BF16)
                normed[row, lane] = (n * ratios[b] * gain_ref[:, lane]).astype(BF16)
        outer_products(1, c, q, dn, 1)
        scatter(1, c)

    outs = {}

    def write(at, src, dst):
        outs[at] = pltpu.make_async_copy(src, dst, out_sem.at[at])
        outs[at].start()

    write(0, normed, normed_hbm)

    def backward(i, _):
        h = i // blocks
        b = lax.rem(i, blocks)
        lane = pl.ds(pl.multiple_of(h * HD, HD), HD)
        r0 = pl.multiple_of(b * BLK, BLK)
        lo, hi, both = pl.ds(r0, HALF), pl.ds(r0 + HALF, HALF), pl.ds(r0, BLK)
        b0 = masked(dot(dn[lo, lane], v[lo, lane], NT), lower(HALF, HALF, 0))
        b1 = masked(dot(dn[hi, lane], v[both, lane], NT), lower(HALF, BLK, HALF))
        s_bf = state[h, b]
        gq[lo, lane] = (dot(b0, k[lo, lane], NN) + dot(dn[lo, lane], s_bf, NT)).astype(BF16)
        gq[hi, lane] = (dot(b1, k[both, lane], NN) + dot(dn[hi, lane], s_bf, NT)).astype(BF16)
        t0 = masked(dot(v[lo, lane], dn[both, lane], NT), upper(HALF, BLK))
        t1 = masked(dot(v[hi, lane], dn[hi, lane], NT), upper(HALF, HALF))
        gk_part[lo, lane] = dot(t0, q[both, lane], NN)
        gk_part[hi, lane] = dot(t1, q[hi, lane], NN)
        gv_part[lo, lane] = dot(a_t[h, b, 0:HALF, :], dn[both, lane], NN)
        gv_part[hi, lane] = dot(a_t[h, b, HALF:BLK, HALF:BLK], dn[hi, lane], NN)
        return 0

    lax.fori_loop(0, heads * blocks, backward, 0)
    write(1, gq, gq_hbm)

    for c in range(chunks):
        scan_and_return(1, c)

    for c in range(chunks):
        wait_exchange(1, 1, c)
        for i in range(2):
            h = 2 * c + i
            lane = slice(h * HD, (h + 1) * HD)
            per = HD // SLICE
            incoming = arrived[1, c, i * per : (i + 1) * per].reshape(HD, HD)
            for b in range(blocks):
                row = slice(b * BLK, (b + 1) * BLK)
                r_bf = (incoming if b == 1 else incoming + first[1, c, i]).astype(BF16)
                gk[row, lane] = (gk_part[row, lane] + dot(v[row, lane], r_bf, NT)).astype(BF16)
                gv[row, lane] = (gv_part[row, lane] + dot(k[row, lane], r_bf, NN)).astype(BF16)
        write(2 + 2 * c, gk.at[:, cols(c)], gk_hbm.at[:, cols(c)])
        write(3 + 2 * c, gv.at[:, cols(c)], gv_hbm.at[:, cols(c)])

    for scan in range(2):
        for phase in range(2):
            for c in range(chunks):
                wait_sent(scan, phase, c)
    stat_wait(stat_send)
    for copy in outs.values():
        copy.wait()


def shards(queries, keys, values, gain, grad_out):
    rows, columns = queries.shape
    heads = columns // HD
    chunks = heads // 2
    blocks = rows // BLK
    n_seq, n_head = lax.axis_size("seq"), lax.axis_size("head")
    out = jax.ShapeDtypeStruct((rows, columns), BF16)
    anywhere = pl.BlockSpec(memory_space=pl.ANY)
    big = pltpu.VMEM((rows, columns), BF16)
    wide = pltpu.VMEM((rows, columns), F32)
    pieces = pltpu.VMEM((2, chunks, n_seq, SLICE, HD), F32)
    flops = heads * blocks * (12 * BLK * BLK * HD + 12 * BLK * HD * HD)
    return pl.pallas_call(
        functools.partial(kernel, n_seq, n_head, columns * n_head),
        out_shape=(out, out, out, out),
        in_specs=[anywhere, anywhere, anywhere, pl.BlockSpec(memory_space=pltpu.VMEM), anywhere],
        out_specs=(anywhere, anywhere, anywhere, anywhere),
        scratch_shapes=[
            big,
            big,
            big,
            big,
            wide,
            big,
            pltpu.VMEM((2, chunks, 2, HD, HD), F32),
            pieces,
            pltpu.VMEM((heads, blocks, HD, HD), BF16),
            pltpu.VMEM((heads, blocks, BLK, BLK), BF16),
            wide,
            wide,
            big,
            big,
            big,
            big,
            pieces,
            pieces,
            pieces,
            pltpu.VMEM((2 * blocks, BLK), F32),
            pltpu.VMEM((n_head, 2 * blocks, BLK), F32),
            pltpu.SemaphoreType.DMA((2 * chunks + 2,)),
            pltpu.SemaphoreType.DMA((2 + 2 * chunks,)),
            pltpu.SemaphoreType.DMA((4 * chunks,)),
            pltpu.SemaphoreType.DMA((4 * chunks,)),
            pltpu.SemaphoreType.DMA,
            pltpu.SemaphoreType.DMA,
        ],
        compiler_params=pltpu.CompilerParams(
            collective_id=0, has_side_effects=True, vmem_limit_bytes=48 << 20
        ),
        cost_estimate=pl.CostEstimate(
            flops=flops, bytes_accessed=8 * rows * columns * 2, transcendentals=0
        ),
    )(queries, keys, values, gain.reshape(1, columns), grad_out)


def solution(mesh):
    spec = P("seq", "head")
    return jax.shard_map(
        shards,
        mesh=mesh,
        in_specs=(spec, spec, spec, P("head"), spec),
        out_specs=(spec, spec, spec, spec),
        check_vma=False,
    )
```

```python
import functools

import jax
import jax.numpy as jnp
from jax import lax
from jax.experimental import pallas as pl
from jax.experimental.pallas import tpu as pltpu
from jax.sharding import PartitionSpec as P

HD = 128
BLK = 512
HALF = BLK // 2
EPS = 1e-06
SLICE = 8
X = 4
CORES = 2
MESH = pl.DeviceIdType.MESH

F32 = jnp.float32
BF16 = jnp.bfloat16

NN = (((1,), (0,)), ((), ()))
NT = (((1,), (1,)), ((), ()))
TN = (((0,), (0,)), ((), ()))


def far_first(me, n, inner):
    outer = n // inner
    major, minor = me // inner, lax.rem(me, inner)

    def hops(step):
        return min(step[0], outer - step[0]) + min(step[1], inner - step[1])

    steps = [(i, j) for i in range(outer) for j in range(inner) if i + j]
    return [
        lax.rem(major + i, outer) * inner + lax.rem(minor + j, inner)
        for i, j in sorted(steps, key=hops, reverse=True)
    ]


def dot(a, b, dims):
    return lax.dot_general(a, b, dims, preferred_element_type=F32)


def lower(rows, columns, offset):
    s = lax.broadcasted_iota(jnp.int32, (rows, columns), 0) + offset
    t = lax.broadcasted_iota(jnp.int32, (rows, columns), 1)
    return t <= s


def upper(rows, columns):
    t = lax.broadcasted_iota(jnp.int32, (rows, columns), 0)
    s = lax.broadcasted_iota(jnp.int32, (rows, columns), 1)
    return t <= s


def masked(scores, mask):
    return jnp.where(mask, scores, 0.0).astype(BF16)


def kernel(
    n_seq,
    n_head,
    width,
    q_hbm,
    k_hbm,
    v_hbm,
    gain_hbm,
    g_hbm,
    normed,
    gq,
    gk_part,
    gv_part,
    k,
    v,
    later,
    q,
    g,
    gain_ref,
    num,
    dn,
    first,
    local,
    state,
    a_t,
    gathered,
    prefix,
    arrived,
    stats,
    all_stats,
    in_sem,
    send_sem,
    recv_sem,
    stat_send,
    stat_recv,
):
    rows, columns = q.shape
    heads = columns // HD
    chunks = heads // 2
    blocks = rows // BLK
    seq = lax.axis_index("seq")
    head = lax.axis_index("head")
    seq_partners = far_first(seq, n_seq, X)
    head_partners = far_first(head, n_head, CORES)

    def cols(c):
        return slice(c * 2 * HD, (c + 1) * 2 * HD)

    barrier = pltpu.get_barrier_semaphore()
    for p in seq_partners:
        pl.semaphore_signal(barrier, inc=1, device_id=(p, head), device_id_type=MESH)
    for p in head_partners:
        pl.semaphore_signal(barrier, inc=1, device_id=(seq, p), device_id_type=MESH)

    loads = {}
    for c in range(chunks):
        for i, (name, src, dst) in enumerate((("k", k_hbm, k), ("v", v_hbm, v))):
            loads[name, c] = pltpu.make_async_copy(
                src.at[:, cols(c)], dst.at[:, cols(c)], in_sem.at[2 * c + i]
            )
            loads[name, c].start()
    for i, (name, src, dst) in enumerate(
        (("q", q_hbm, q), ("g", g_hbm, g), ("gain", gain_hbm, gain_ref))
    ):
        loads[name] = pltpu.make_async_copy(src, dst, in_sem.at[2 * chunks + i])
        loads[name].start()

    def exchange(scan, phase, c, source, landing):
        at = ((scan * 2) + phase) * chunks + c
        for p in seq_partners:
            pltpu.make_async_remote_copy(
                src_ref=source(p),
                dst_ref=landing,
                send_sem=send_sem.at[at],
                recv_sem=recv_sem.at[at],
                device_id=(p, head),
                device_id_type=MESH,
            ).start()

    def wait_exchange(scan, phase, c):
        at = ((scan * 2) + phase) * chunks + c
        n = n_seq - 1
        pltpu.make_async_copy(
            gathered.at[scan, c, pl.ds(0, n)],
            gathered.at[scan, c, pl.ds(0, n)],
            recv_sem.at[at],
        ).wait()

    def wait_sent(scan, phase, c):
        at = ((scan * 2) + phase) * chunks + c
        n = n_seq - 1
        pltpu.make_async_copy(
            gathered.at[scan, c, pl.ds(0, n)],
            gathered.at[scan, c, pl.ds(0, n)],
            send_sem.at[at],
        ).wait()

    def scatter(scan, c):
        gathered[scan, c, seq] = local[scan, c, seq]
        exchange(
            scan, 0, c, lambda p: local.at[scan, c, p], gathered.at[scan, c, seq]
        )

    def scan_and_return(scan, c):
        wait_exchange(scan, 0, c)
        total = jnp.zeros((SLICE, HD), F32)
        order = range(n_seq) if scan == 0 else range(n_seq - 1, -1, -1)
        for j in order:
            prefix[scan, c, j] = total
            total = total + gathered[scan, c, j]
        arrived[scan, c, seq] = prefix[scan, c, seq]
        exchange(
            scan, 1, c, lambda p: prefix.at[scan, c, p], arrived.at[scan, c, seq]
        )

    def outer_products(scan, c, left, right, keep):
        for i in range(2):
            h = 2 * c + i
            lane = slice(h * HD, (h + 1) * HD)
            parts = [
                dot(left[b * BLK : (b + 1) * BLK, lane], right[b * BLK : (b + 1) * BLK, lane], TN)
                for b in range(blocks)
            ]
            first[scan, c, i] = parts[keep]
            per = HD // SLICE
            local[scan, c, i * per : (i + 1) * per] = (parts[0] + parts[1]).reshape(
                per, SLICE, HD
            )

    for c in range(chunks):
        loads["k", c].wait()
        loads["v", c].wait()
        outer_products(0, c, k, v, 0)
        if c == 0:
            pl.semaphore_wait(barrier, n_seq - 1 + n_head - 1)
        scatter(0, c)

    loads["q"].wait()

    def scores(i, _):
        h = i // blocks
        b = lax.rem(i, blocks)
        lane = pl.ds(pl.multiple_of(h * HD, HD), HD)
        r0 = pl.multiple_of(b * BLK, BLK)
        lo, hi, both = pl.ds(r0, HALF), pl.ds(r0 + HALF, HALF), pl.ds(r0, BLK)
        a0 = masked(dot(q[lo, lane], k[lo, lane], NT), lower(HALF, HALF, 0))
        a1 = masked(dot(q[hi, lane], k[both, lane], NT), lower(HALF, BLK, HALF))
        num[lo, lane] = dot(a0, v[lo, lane], NN)
        num[hi, lane] = dot(a1, v[both, lane], NN)
        t0 = masked(dot(k[lo, lane], q[both, lane], NT), upper(HALF, BLK))
        t1 = masked(dot(k[hi, lane], q[hi, lane], NT), upper(HALF, HALF))
        a_t[h, b, 0:HALF, :] = t0
        a_t[h, b, HALF:BLK, HALF:BLK] = t1
        return 0

    lax.fori_loop(0, heads * blocks, scores, 0)

    for c in range(chunks):
        scan_and_return(0, c)

    loads["g"].wait()
    loads["gain"].wait()
    square = [None] * blocks
    product = [None] * blocks
    for c in range(chunks):
        wait_exchange(0, 1, c)
        for i in range(2):
            h = 2 * c + i
            lane = slice(h * HD, (h + 1) * HD)
            per = HD // SLICE
            incoming = arrived[0, c, i * per : (i + 1) * per].reshape(HD, HD)
            for b in range(blocks):
                row = slice(b * BLK, (b + 1) * BLK)
                s_bf = (incoming if b == 0 else incoming + first[0, c, i]).astype(BF16)
                state[h, b] = s_bf
                n = num[row, lane] + dot(q[row, lane], s_bf, NN)
                num[row, lane] = n
                gn = g[row, lane].astype(F32) * gain_ref[:, lane]
                sq, pr = n * n, gn * n
                square[b] = sq if square[b] is None else square[b] + sq
                product[b] = pr if product[b] is None else product[b] + pr

    ones = jnp.ones((SLICE, HD), BF16)

    def across(x):
        hi = x.astype(BF16)
        rest = x - hi.astype(F32)
        mid = rest.astype(BF16)
        low = (rest - mid.astype(F32)).astype(BF16)
        return (dot(ones, hi, NT) + dot(ones, mid, NT) + dot(ones, low, NT))[0:1]

    for b in range(blocks):
        stats[b : b + 1, :] = across(square[b])
        stats[blocks + b : blocks + b + 1, :] = across(product[b])
    all_stats[head] = stats[...]
    for p in head_partners:
        pltpu.make_async_remote_copy(
            src_ref=stats,
            dst_ref=all_stats.at[head],
            send_sem=stat_send,
            recv_sem=stat_recv,
            device_id=(seq, p),
            device_id_type=MESH,
        ).start()

    def stat_wait(sem):
        view = all_stats.at[pl.ds(0, n_head - 1)]
        pltpu.make_async_copy(view, view, sem).wait()

    stat_wait(stat_recv)
    totals = all_stats[0]
    for j in range(1, n_head):
        totals = totals + all_stats[j]
    ratio = lax.rsqrt(totals[0:blocks] / width + EPS)
    inner = totals[blocks:] / width
    weight = ratio * ratio * inner
    packed = jnp.concatenate([ratio, weight, jnp.zeros((8 - 2 * blocks, BLK), F32)], axis=0)
    turned = jnp.transpose(packed)
    ratios = [jnp.broadcast_to(turned[:, b : b + 1], (BLK, HD)) for b in range(blocks)]
    weights = [
        jnp.broadcast_to(turned[:, blocks + b : blocks + b + 1], (BLK, HD))
        for b in range(blocks)
    ]

    for c in range(chunks):
        for i in range(2):
            lane = slice((2 * c + i) * HD, (2 * c + i + 1) * HD)
            for b in range(blocks):
                row = slice(b * BLK, (b + 1) * BLK)
                n = num[row, lane]
                gn = g[row, lane].astype(F32) * gain_ref[:, lane]
                dn[row, lane] = (ratios[b] * (gn - weights[b] * n)).astype(BF16)
                normed[row, lane] = (n * ratios[b] * gain_ref[:, lane]).astype(BF16)
        outer_products(1, c, q, dn, 1)
        scatter(1, c)

    def backward(i, _):
        h = i // blocks
        b = lax.rem(i, blocks)
        lane = pl.ds(pl.multiple_of(h * HD, HD), HD)
        r0 = pl.multiple_of(b * BLK, BLK)
        lo, hi, both = pl.ds(r0, HALF), pl.ds(r0 + HALF, HALF), pl.ds(r0, BLK)
        b0 = masked(dot(dn[lo, lane], v[lo, lane], NT), lower(HALF, HALF, 0))
        b1 = masked(dot(dn[hi, lane], v[both, lane], NT), lower(HALF, BLK, HALF))
        s_bf = state[h, b]
        gq[lo, lane] = (dot(b0, k[lo, lane], NN) + dot(dn[lo, lane], s_bf, NT)).astype(BF16)
        gq[hi, lane] = (dot(b1, k[both, lane], NN) + dot(dn[hi, lane], s_bf, NT)).astype(BF16)
        t0 = masked(dot(v[lo, lane], dn[both, lane], NT), upper(HALF, BLK))
        t1 = masked(dot(v[hi, lane], dn[hi, lane], NT), upper(HALF, HALF))
        gk_part[lo, lane] = dot(t0, q[both, lane], NN)
        gk_part[hi, lane] = dot(t1, q[hi, lane], NN)
        gv_part[lo, lane] = dot(a_t[h, b, 0:HALF, :], dn[both, lane], NN)
        gv_part[hi, lane] = dot(a_t[h, b, HALF:BLK, HALF:BLK], dn[hi, lane], NN)
        return 0

    lax.fori_loop(0, heads * blocks // 2, backward, 0)

    for c in range(chunks):
        scan_and_return(1, c)

    lax.fori_loop(heads * blocks // 2, heads * blocks, backward, 0)

    for c in range(chunks):
        wait_exchange(1, 1, c)
        for i in range(2):
            per = HD // SLICE
            incoming = arrived[1, c, i * per : (i + 1) * per].reshape(HD, HD)
            for b in range(blocks):
                r = incoming if b == 1 else incoming + first[1, c, i]
                later[2 * c + i, b] = r.astype(BF16)

    for scan in range(2):
        for phase in range(2):
            for c in range(chunks):
                wait_sent(scan, phase, c)
    stat_wait(stat_send)


def finish(
    normed,
    gq,
    gk_part,
    gv_part,
    k,
    v,
    later,
    normed_hbm,
    gq_hbm,
    gk_hbm,
    gv_hbm,
    gk,
    gv,
    out_sem,
):
    rows, columns = k.shape
    blocks = rows // BLK
    outs = []

    def write(src, dst):
        outs.append(pltpu.make_async_copy(src, dst, out_sem.at[len(outs)]))
        outs[-1].start()

    write(normed, normed_hbm)
    write(gq, gq_hbm)
    for h in range(columns // HD):
        lane = slice(h * HD, (h + 1) * HD)
        for b in range(blocks):
            row = slice(b * BLK, (b + 1) * BLK)
            gk[row, lane] = (gk_part[row, lane] + dot(v[row, lane], later[h, b], NT)).astype(BF16)
            gv[row, lane] = (gv_part[row, lane] + dot(k[row, lane], later[h, b], NN)).astype(BF16)
        if h % 2 == 1:
            pair = slice((h - 1) * HD, (h + 1) * HD)
            write(gk.at[:, pair], gk_hbm.at[:, pair])
            write(gv.at[:, pair], gv_hbm.at[:, pair])
    for copy in outs:
        copy.wait()


def shards(queries, keys, values, gain, grad_out):
    rows, columns = queries.shape
    heads = columns // HD
    chunks = heads // 2
    blocks = rows // BLK
    n_seq, n_head = lax.axis_size("seq"), lax.axis_size("head")
    out = jax.ShapeDtypeStruct((rows, columns), BF16)
    anywhere = pl.BlockSpec(memory_space=pl.ANY)
    big = pltpu.VMEM((rows, columns), BF16)
    wide = pltpu.VMEM((rows, columns), F32)
    pieces = pltpu.VMEM((2, chunks, n_seq, SLICE, HD), F32)
    flops = heads * blocks * (12 * BLK * BLK * HD + 12 * BLK * HD * HD)
    vmem = pl.BlockSpec(memory_space=pltpu.VMEM)
    hbm = [
        pltpu.with_memory_space_constraint(x, pltpu.HBM)
        for x in (queries, keys, values, gain.reshape(1, columns), grad_out)
    ]
    kept = (
        pltpu.VMEM((rows, columns), BF16),
        pltpu.VMEM((rows, columns), BF16),
        pltpu.VMEM((rows, columns), F32),
        pltpu.VMEM((rows, columns), F32),
        pltpu.VMEM((rows, columns), BF16),
        pltpu.VMEM((rows, columns), BF16),
        pltpu.VMEM((heads, blocks, HD, HD), BF16),
    )
    held = pl.pallas_call(
        functools.partial(kernel, n_seq, n_head, columns * n_head),
        out_shape=kept,
        in_specs=[anywhere] * 5,
        out_specs=(vmem,) * len(kept),
        scratch_shapes=[
            big,
            big,
            pltpu.VMEM((1, columns), F32),
            wide,
            big,
            pltpu.VMEM((2, chunks, 2, HD, HD), F32),
            pieces,
            pltpu.VMEM((heads, blocks, HD, HD), BF16),
            pltpu.VMEM((heads, blocks, BLK, BLK), BF16),
            pieces,
            pieces,
            pieces,
            pltpu.VMEM((2 * blocks, BLK), F32),
            pltpu.VMEM((n_head, 2 * blocks, BLK), F32),
            pltpu.SemaphoreType.DMA((2 * chunks + 3,)),
            pltpu.SemaphoreType.DMA((4 * chunks,)),
            pltpu.SemaphoreType.DMA((4 * chunks,)),
            pltpu.SemaphoreType.DMA,
            pltpu.SemaphoreType.DMA,
        ],
        compiler_params=pltpu.CompilerParams(
            collective_id=0, has_side_effects=True, vmem_limit_bytes=32 << 20
        ),
        cost_estimate=pl.CostEstimate(
            flops=flops, bytes_accessed=4 * rows * columns * 2, transcendentals=0
        ),
    )(*hbm)
    return pl.pallas_call(
        finish,
        out_shape=(out, out, out, out),
        in_specs=[vmem] * len(kept),
        out_specs=(anywhere,) * 4,
        scratch_shapes=[big, big, pltpu.SemaphoreType.DMA((2 + 2 * chunks,))],
        compiler_params=pltpu.CompilerParams(vmem_limit_bytes=24 << 20),
        cost_estimate=pl.CostEstimate(
            flops=heads * blocks * 4 * BLK * HD * HD,
            bytes_accessed=4 * rows * columns * 2,
            transcendentals=0,
        ),
    )(*held)


def solution(mesh):
    spec = P("seq", "head")
    return jax.shard_map(
        shards,
        mesh=mesh,
        in_specs=(spec, spec, spec, P("head"), spec),
        out_specs=(spec, spec, spec, spec),
        check_vma=False,
    )
```

```python
import functools

import jax
import jax.numpy as jnp
from jax import lax
from jax.experimental import pallas as pl
from jax.experimental.pallas import tpu as pltpu
from jax.sharding import PartitionSpec as P

HD = 128
BLK = 512
HALF = BLK // 2
EPS = 1e-06
SLICE = 8
X = 4
CORES = 2
MESH = pl.DeviceIdType.MESH

F32 = jnp.float32
BF16 = jnp.bfloat16

NN = (((1,), (0,)), ((), ()))
NT = (((1,), (1,)), ((), ()))
TN = (((0,), (0,)), ((), ()))


def far_first(me, n, inner):
    outer = n // inner
    major, minor = me // inner, lax.rem(me, inner)

    def hops(step):
        return min(step[0], outer - step[0]) + min(step[1], inner - step[1])

    steps = [(i, j) for i in range(outer) for j in range(inner) if i + j]
    return [
        lax.rem(major + i, outer) * inner + lax.rem(minor + j, inner)
        for i, j in sorted(steps, key=hops, reverse=True)
    ]


def dot(a, b, dims):
    return lax.dot_general(a, b, dims, preferred_element_type=F32)


def lower(rows, columns, offset):
    s = lax.broadcasted_iota(jnp.int32, (rows, columns), 0) + offset
    t = lax.broadcasted_iota(jnp.int32, (rows, columns), 1)
    return t <= s


def upper(rows, columns):
    t = lax.broadcasted_iota(jnp.int32, (rows, columns), 0)
    s = lax.broadcasted_iota(jnp.int32, (rows, columns), 1)
    return t <= s


def masked(scores, mask):
    return jnp.where(mask, scores, 0.0).astype(BF16)


def last_products(row, lane, r, v, k, gk_part, gv_part, gk, gv):
    gk[row, lane] = (gk_part[row, lane] + dot(v[row, lane], r, NT)).astype(BF16)
    gv[row, lane] = (gv_part[row, lane] + dot(k[row, lane], r, NN)).astype(BF16)


def kernel(
    n_seq,
    n_head,
    width,
    q_hbm,
    k_hbm,
    v_hbm,
    gain_hbm,
    g_hbm,
    normed,
    gq,
    gk,
    gv,
    gk_part,
    gv_part,
    k,
    v,
    later,
    q,
    g,
    gain_ref,
    gn,
    q_t,
    num,
    dn,
    first,
    local,
    state,
    pair,
    a_t,
    gathered,
    prefix,
    arrived,
    stats,
    all_stats,
    in_sem,
    send_sem,
    recv_sem,
    stat_send,
    stat_recv,
):
    rows, columns = q.shape
    heads = columns // HD
    chunks = heads // 2
    blocks = rows // BLK
    seq = lax.axis_index("seq")
    head = lax.axis_index("head")
    seq_partners = far_first(seq, n_seq, X)
    head_partners = far_first(head, n_head, CORES)

    def cols(c):
        return slice(c * 2 * HD, (c + 1) * 2 * HD)

    barrier = pltpu.get_barrier_semaphore()
    for p in seq_partners:
        pl.semaphore_signal(barrier, inc=1, device_id=(p, head), device_id_type=MESH)
    for p in head_partners:
        pl.semaphore_signal(barrier, inc=1, device_id=(seq, p), device_id_type=MESH)

    loads = {}
    for c in range(chunks):
        for i, (name, src, dst) in enumerate((("k", k_hbm, k), ("v", v_hbm, v))):
            loads[name, c] = pltpu.make_async_copy(
                src.at[:, cols(c)], dst.at[:, cols(c)], in_sem.at[2 * c + i]
            )
            loads[name, c].start()
    for i, (name, src, dst) in enumerate(
        (("q", q_hbm, q), ("g", g_hbm, g), ("gain", gain_hbm, gain_ref))
    ):
        loads[name] = pltpu.make_async_copy(src, dst, in_sem.at[2 * chunks + i])
        loads[name].start()

    def exchange(scan, phase, c, source, landing):
        at = ((scan * 2) + phase) * chunks + c
        for p in seq_partners:
            pltpu.make_async_remote_copy(
                src_ref=source(p),
                dst_ref=landing,
                send_sem=send_sem.at[at],
                recv_sem=recv_sem.at[at],
                device_id=(p, head),
                device_id_type=MESH,
            ).start()

    def wait_exchange(scan, phase, c):
        at = ((scan * 2) + phase) * chunks + c
        n = n_seq - 1
        pltpu.make_async_copy(
            gathered.at[scan, c, pl.ds(0, n)],
            gathered.at[scan, c, pl.ds(0, n)],
            recv_sem.at[at],
        ).wait()

    def wait_sent(scan, phase, c):
        at = ((scan * 2) + phase) * chunks + c
        n = n_seq - 1
        pltpu.make_async_copy(
            gathered.at[scan, c, pl.ds(0, n)],
            gathered.at[scan, c, pl.ds(0, n)],
            send_sem.at[at],
        ).wait()

    def scatter(scan, c):
        gathered[scan, c, seq] = local[scan, c, seq]
        exchange(
            scan, 0, c, lambda p: local.at[scan, c, p], gathered.at[scan, c, seq]
        )

    def scan_and_return(scan, c):
        wait_exchange(scan, 0, c)
        total = jnp.zeros((SLICE, HD), F32)
        order = range(n_seq) if scan == 0 else range(n_seq - 1, -1, -1)
        for j in order:
            prefix[scan, c, j] = total
            total = total + gathered[scan, c, j]
        arrived[scan, c, seq] = prefix[scan, c, seq]
        exchange(
            scan, 1, c, lambda p: prefix.at[scan, c, p], arrived.at[scan, c, seq]
        )

    def place_states(scan, c, b, plain):
        per = HD // SLICE
        for i in range(2):
            at = slice(i * HD, (i + 1) * HD)
            s = arrived[scan, c, i * per : (i + 1) * per].reshape(HD, HD)
            s = s if plain else s + first[scan, c, i]
            pair[scan, c, b, at, at] = s.astype(BF16)

    def outer_products(scan, c, product_of, keep):
        for i in range(2):
            h = 2 * c + i
            parts = [product_of(h, b) for b in range(blocks)]
            first[scan, c, i] = parts[keep]
            per = HD // SLICE
            local[scan, c, i * per : (i + 1) * per] = (parts[0] + parts[1]).reshape(
                per, SLICE, HD
            )

    def tile(h, b):
        return slice(b * BLK, (b + 1) * BLK), slice(h * HD, (h + 1) * HD)

    def kv_product(h, b):
        return dot(k[tile(h, b)], v[tile(h, b)], TN)

    def qd_product(h, b):
        row, lane = tile(h, b)
        return dot(q_t[lane, row], dn[row, lane], NN)

    pair[...] = jnp.zeros_like(pair)
    for c in range(chunks):
        loads["k", c].wait()
        loads["v", c].wait()
        outer_products(0, c, kv_product, 0)
        if c == 0:
            pl.semaphore_wait(barrier, n_seq - 1 + n_head - 1)
        scatter(0, c)

    loads["q"].wait()

    def scores(i, _):
        h = i // blocks
        b = lax.rem(i, blocks)
        lane = pl.ds(pl.multiple_of(h * HD, HD), HD)
        r0 = pl.multiple_of(b * BLK, BLK)
        lo, hi, both = pl.ds(r0, HALF), pl.ds(r0 + HALF, HALF), pl.ds(r0, BLK)
        a0 = masked(dot(q[lo, lane], k[lo, lane], NT), lower(HALF, HALF, 0))
        a1 = masked(dot(q[hi, lane], k[both, lane], NT), lower(HALF, BLK, HALF))
        num[lo, lane] = dot(a0, v[lo, lane], NN)
        num[hi, lane] = dot(a1, v[both, lane], NN)
        t0 = masked(dot(k[lo, lane], q[both, lane], NT), upper(HALF, BLK))
        t1 = masked(dot(k[hi, lane], q[hi, lane], NT), upper(HALF, HALF))
        q_t[lane, both] = jnp.transpose(q[both, lane])
        a_t[h, b, 0:HALF, :] = t0
        a_t[h, b, HALF:BLK, HALF:BLK] = t1
        return 0

    lax.fori_loop(0, heads * blocks, scores, 0)

    for c in range(chunks):
        scan_and_return(0, c)

    loads["g"].wait()
    loads["gain"].wait()
    gn[...] = g[...].astype(F32) * gain_ref[...]
    square = [None] * blocks
    product = [None] * blocks
    for c in range(chunks):
        wait_exchange(0, 1, c)
        for b in range(blocks):
            place_states(0, c, b, b == 0)
            for i in range(2):
                at = slice(i * HD, (i + 1) * HD)
                state[2 * c + i, b] = pair[0, c, b, at, at]
            row = slice(b * BLK, (b + 1) * BLK)
            n = num[row, cols(c)] + dot(q[row, cols(c)], pair[0, c, b], NN)
            num[row, cols(c)] = n
            sq, pr = n * n, gn[row, cols(c)] * n
            sq, pr = sq[:, :HD] + sq[:, HD:], pr[:, :HD] + pr[:, HD:]
            square[b] = sq if c == 0 else square[b] + sq
            product[b] = pr if c == 0 else product[b] + pr

    lanes = lax.broadcasted_iota(jnp.int32, (BLK, HD), 1)
    mixed = jnp.zeros((BLK, HD), F32)
    for at, x in enumerate(square + product):
        mixed = jnp.where(lanes == at, jnp.sum(x, axis=1, keepdims=True), mixed)
    stats[...] = jnp.transpose(mixed)[0 : 2 * blocks]
    all_stats[head] = stats[...]
    for p in head_partners:
        pltpu.make_async_remote_copy(
            src_ref=stats,
            dst_ref=all_stats.at[head],
            send_sem=stat_send,
            recv_sem=stat_recv,
            device_id=(seq, p),
            device_id_type=MESH,
        ).start()

    def stat_wait(sem):
        view = all_stats.at[pl.ds(0, n_head - 1)]
        pltpu.make_async_copy(view, view, sem).wait()

    stat_wait(stat_recv)
    totals = all_stats[0]
    for j in range(1, n_head):
        totals = totals + all_stats[j]
    ratio = lax.rsqrt(totals[0:blocks] / width + EPS)
    inner = totals[blocks:] / width
    weight = ratio * ratio * inner
    packed = jnp.concatenate([ratio, weight, jnp.zeros((8 - 2 * blocks, BLK), F32)], axis=0)
    turned = jnp.transpose(packed)
    ratios = [jnp.broadcast_to(turned[:, b : b + 1], (BLK, HD)) for b in range(blocks)]
    weights = [
        jnp.broadcast_to(turned[:, blocks + b : blocks + b + 1], (BLK, HD))
        for b in range(blocks)
    ]

    for c in range(chunks):
        for i in range(2):
            for b in range(blocks):
                at = tile(2 * c + i, b)
                dn[at] = (ratios[b] * (gn[at] - weights[b] * num[at])).astype(BF16)
        outer_products(1, c, qd_product, 1)
        scatter(1, c)

    for h in range(heads):
        for b in range(blocks):
            row, lane = tile(h, b)
            normed[row, lane] = (num[row, lane] * ratios[b] * gain_ref[:, lane]).astype(BF16)

    def backward(i, _):
        h = i // blocks
        b = lax.rem(i, blocks)
        lane = pl.ds(pl.multiple_of(h * HD, HD), HD)
        r0 = pl.multiple_of(b * BLK, BLK)
        lo, hi, both = pl.ds(r0, HALF), pl.ds(r0 + HALF, HALF), pl.ds(r0, BLK)
        b0 = masked(dot(dn[lo, lane], v[lo, lane], NT), lower(HALF, HALF, 0))
        b1 = masked(dot(dn[hi, lane], v[both, lane], NT), lower(HALF, BLK, HALF))
        s_bf = state[h, b]
        gq[lo, lane] = (dot(b0, k[lo, lane], NN) + dot(dn[lo, lane], s_bf, NT)).astype(BF16)
        gq[hi, lane] = (dot(b1, k[both, lane], NN) + dot(dn[hi, lane], s_bf, NT)).astype(BF16)
        t0 = masked(dot(v[lo, lane], dn[both, lane], NT), upper(HALF, BLK))
        t1 = masked(dot(v[hi, lane], dn[hi, lane], NT), upper(HALF, HALF))
        gk_part[lo, lane] = dot(t0, q[both, lane], NN)
        gk_part[hi, lane] = dot(t1, q[hi, lane], NN)
        gv_part[lo, lane] = dot(a_t[h, b, 0:HALF, :], dn[both, lane], NN)
        gv_part[hi, lane] = dot(a_t[h, b, HALF:BLK, HALF:BLK], dn[hi, lane], NN)
        return 0

    lax.fori_loop(0, heads * blocks // 2, backward, 0)

    for c in range(chunks):
        scan_and_return(1, c)

    lax.fori_loop(heads * blocks // 2, heads * blocks, backward, 0)

    for c in range(chunks):
        wait_exchange(1, 1, c)
        for b in range(blocks):
            place_states(1, c, b, b == blocks - 1)
            if c < chunks - 1:
                row = slice(b * BLK, (b + 1) * BLK)
                last_products(
                    row, cols(c), pair[1, c, b], v, k, gk_part, gv_part, gk, gv
                )
            else:
                later[b] = pair[1, c, b]

    for scan in range(2):
        for phase in range(2):
            for c in range(chunks):
                wait_sent(scan, phase, c)
    stat_wait(stat_send)


def finish(
    normed,
    gq,
    gk_done,
    gv_done,
    gk_part,
    gv_part,
    k,
    v,
    later,
    normed_hbm,
    gq_hbm,
    gk_hbm,
    gv_hbm,
    gk,
    gv,
    out_sem,
):
    rows, columns = k.shape
    blocks = rows // BLK
    done = slice(0, columns - 2 * HD)
    rest = slice(columns - 2 * HD, columns)
    outs = []

    def write(src, dst):
        outs.append(pltpu.make_async_copy(src, dst, out_sem.at[len(outs)]))
        outs[-1].start()

    write(normed, normed_hbm)
    write(gq, gq_hbm)
    write(gk_done.at[:, done], gk_hbm.at[:, done])
    write(gv_done.at[:, done], gv_hbm.at[:, done])
    for b in range(blocks):
        row = slice(b * BLK, (b + 1) * BLK)
        last_products(row, rest, later[b], v, k, gk_part, gv_part, gk, gv)
        write(gk.at[row, rest], gk_hbm.at[row, rest])
        write(gv.at[row, rest], gv_hbm.at[row, rest])
    for copy in outs:
        copy.wait()


def shards(queries, keys, values, gain, grad_out):
    rows, columns = queries.shape
    heads = columns // HD
    chunks = heads // 2
    blocks = rows // BLK
    n_seq, n_head = lax.axis_size("seq"), lax.axis_size("head")
    out = jax.ShapeDtypeStruct((rows, columns), BF16)
    anywhere = pl.BlockSpec(memory_space=pl.ANY)
    big = pltpu.VMEM((rows, columns), BF16)
    wide = pltpu.VMEM((rows, columns), F32)
    pieces = pltpu.VMEM((2, chunks, n_seq, SLICE, HD), F32)
    flops = heads * blocks * (12 * BLK * BLK * HD + 12 * BLK * HD * HD)
    vmem = pl.BlockSpec(memory_space=pltpu.VMEM)
    hbm = [
        pltpu.with_memory_space_constraint(x, pltpu.HBM)
        for x in (queries, keys, values, gain.reshape(1, columns), grad_out)
    ]
    kept = (
        pltpu.VMEM((rows, columns), BF16),
        pltpu.VMEM((rows, columns), BF16),
        pltpu.VMEM((rows, columns), BF16),
        pltpu.VMEM((rows, columns), BF16),
        pltpu.VMEM((rows, columns), F32),
        pltpu.VMEM((rows, columns), F32),
        pltpu.VMEM((rows, columns), BF16),
        pltpu.VMEM((rows, columns), BF16),
        pltpu.VMEM((blocks, 2 * HD, 2 * HD), BF16),
    )
    held = pl.pallas_call(
        functools.partial(kernel, n_seq, n_head, columns * n_head),
        out_shape=kept,
        in_specs=[anywhere] * 5,
        out_specs=(vmem,) * len(kept),
        scratch_shapes=[
            big,
            big,
            pltpu.VMEM((1, columns), F32),
            wide,
            pltpu.VMEM((columns, rows), BF16),
            wide,
            big,
            pltpu.VMEM((2, chunks, 2, HD, HD), F32),
            pieces,
            pltpu.VMEM((heads, blocks, HD, HD), BF16),
            pltpu.VMEM((2, chunks, blocks, 2 * HD, 2 * HD), BF16),
            pltpu.VMEM((heads, blocks, BLK, BLK), BF16),
            pieces,
            pieces,
            pieces,
            pltpu.VMEM((2 * blocks, BLK), F32),
            pltpu.VMEM((n_head, 2 * blocks, BLK), F32),
            pltpu.SemaphoreType.DMA((2 * chunks + 3,)),
            pltpu.SemaphoreType.DMA((4 * chunks,)),
            pltpu.SemaphoreType.DMA((4 * chunks,)),
            pltpu.SemaphoreType.DMA,
            pltpu.SemaphoreType.DMA,
        ],
        compiler_params=pltpu.CompilerParams(
            collective_id=0, has_side_effects=True, vmem_limit_bytes=32 << 20
        ),
        cost_estimate=pl.CostEstimate(
            flops=flops, bytes_accessed=4 * rows * columns * 2, transcendentals=0
        ),
    )(*hbm)
    return pl.pallas_call(
        finish,
        out_shape=(out, out, out, out),
        in_specs=[vmem] * len(kept),
        out_specs=(anywhere,) * 4,
        scratch_shapes=[big, big, pltpu.SemaphoreType.DMA((4 + 2 * blocks,))],
        compiler_params=pltpu.CompilerParams(vmem_limit_bytes=24 << 20),
        cost_estimate=pl.CostEstimate(
            flops=heads * blocks * 4 * BLK * HD * HD,
            bytes_accessed=4 * rows * columns * 2,
            transcendentals=0,
        ),
    )(*held)


def solution(mesh):
    spec = P("seq", "head")
    return jax.shard_map(
        shards,
        mesh=mesh,
        in_specs=(spec, spec, spec, P("head"), spec),
        out_specs=(spec, spec, spec, spec),
        check_vma=False,
    )
```

```python
import functools

import jax
import jax.numpy as jnp
from jax import lax
from jax.experimental import pallas as pl
from jax.experimental.pallas import tpu as pltpu
from jax.sharding import PartitionSpec as P

HD = 128
BLK = 512
HALF = BLK // 2
EPS = 1e-06
GROUP = 8
SLICE = 2 * HD // GROUP
X = 4
CORES = 2
MESH = pl.DeviceIdType.MESH

F32 = jnp.float32
BF16 = jnp.bfloat16

NN = (((1,), (0,)), ((), ()))
NT = (((1,), (1,)), ((), ()))
TN = (((0,), (0,)), ((), ()))


def far_first(me, n, inner):
    outer = n // inner
    major, minor = me // inner, lax.rem(me, inner)

    def hops(step):
        return min(step[0], outer - step[0]) + min(step[1], inner - step[1])

    steps = [(i, j) for i in range(outer) for j in range(inner) if i + j]
    return [
        lax.rem(major + i, outer) * inner + lax.rem(minor + j, inner)
        for i, j in sorted(steps, key=hops, reverse=True)
    ]


def dot(a, b, dims):
    return lax.dot_general(a, b, dims, preferred_element_type=F32)


def lower(rows, columns, offset):
    s = lax.broadcasted_iota(jnp.int32, (rows, columns), 0) + offset
    t = lax.broadcasted_iota(jnp.int32, (rows, columns), 1)
    return t <= s


def upper(rows, columns):
    t = lax.broadcasted_iota(jnp.int32, (rows, columns), 0)
    s = lax.broadcasted_iota(jnp.int32, (rows, columns), 1)
    return t <= s


def masked(scores, mask):
    return jnp.where(mask, scores, 0.0).astype(BF16)


def last_products(row, lane, r, v, k, gk_part, gv_part, gk, gv):
    gk[row, lane] = (gk_part[row, lane] + dot(v[row, lane], r, NT)).astype(BF16)
    gv[row, lane] = (gv_part[row, lane] + dot(k[row, lane], r, NN)).astype(BF16)


def kernel(
    n_seq,
    n_head,
    width,
    q_hbm,
    k_hbm,
    v_hbm,
    gain_hbm,
    g_hbm,
    normed,
    gq,
    gk,
    gv,
    gk_part,
    gv_part,
    k,
    v,
    later,
    q,
    g,
    gain_ref,
    gn,
    q_t,
    num,
    dn,
    first,
    local,
    state,
    pair,
    a_t,
    gathered,
    prefix,
    arrived,
    totals,
    stats,
    all_stats,
    in_sem,
    send_sem,
    recv_sem,
    stat_send,
    stat_recv,
):
    rows, columns = q.shape
    heads = columns // HD
    chunks = heads // 2
    blocks = rows // BLK
    seq = lax.axis_index("seq")
    head = lax.axis_index("head")
    n_group = n_seq // GROUP
    group, member = seq // GROUP, lax.rem(seq, GROUP)
    near_partners = far_first(member, GROUP, X)
    far_partners = far_first(group, n_group, 1)
    head_partners = far_first(head, n_head, CORES)

    def cols(c):
        return slice(c * 2 * HD, (c + 1) * 2 * HD)

    barrier = pltpu.get_barrier_semaphore()
    for p in far_partners:
        to = (p * GROUP + member, head)
        pl.semaphore_signal(barrier, inc=1, device_id=to, device_id_type=MESH)
    for p in near_partners:
        to = (group * GROUP + p, head)
        pl.semaphore_signal(barrier, inc=1, device_id=to, device_id_type=MESH)
    for p in head_partners:
        pl.semaphore_signal(barrier, inc=1, device_id=(seq, p), device_id_type=MESH)

    loads = {}
    for c in range(chunks):
        for i, (name, src, dst) in enumerate((("k", k_hbm, k), ("v", v_hbm, v))):
            loads[name, c] = pltpu.make_async_copy(
                src.at[:, cols(c)], dst.at[:, cols(c)], in_sem.at[2 * c + i]
            )
            loads[name, c].start()
    for i, (name, src, dst) in enumerate(
        (("q", q_hbm, q), ("g", g_hbm, g), ("gain", gain_hbm, gain_ref))
    ):
        loads[name] = pltpu.make_async_copy(src, dst, in_sem.at[2 * chunks + i])
        loads[name].start()

    def sems(scan, phase, c):
        return (scan * 3 + phase) * chunks + c

    def send(scan, phase, c, source, landing, to):
        at = sems(scan, phase, c)
        pltpu.make_async_remote_copy(
            src_ref=source,
            dst_ref=landing,
            send_sem=send_sem.at[at],
            recv_sem=recv_sem.at[at],
            device_id=(to, head),
            device_id_type=MESH,
        ).start()

    def wait_for(sem, scan, phase, c):
        n = (n_group if phase == 1 else GROUP) - 1
        view = gathered.at[scan, c, pl.ds(0, n)]
        pltpu.make_async_copy(view, view, sem.at[sems(scan, phase, c)]).wait()

    def wait_exchange(scan, phase, c):
        wait_for(recv_sem, scan, phase, c)

    def wait_sent(scan, phase, c):
        wait_for(send_sem, scan, phase, c)

    def scatter(scan, c):
        landing = gathered.at[scan, c, member]
        for p in near_partners:
            send(scan, 0, c, local.at[scan, c, p], landing, group * GROUP + p)
        gathered[scan, c, member] = local[scan, c, member]

    def share_totals(scan, c):
        wait_exchange(scan, 0, c)
        sum_here = jnp.zeros((SLICE, HD), F32)
        for j in range(GROUP) if scan == 0 else range(GROUP - 1, -1, -1):
            prefix[scan, c, j] = sum_here
            sum_here = sum_here + gathered[scan, c, j]
        totals[scan, c, group] = sum_here
        mine = totals.at[scan, c, group]
        for p in far_partners:
            send(scan, 1, c, mine, mine, p * GROUP + member)

    def hand_back(scan, c):
        wait_exchange(scan, 1, c)
        outside = jnp.zeros((SLICE, HD), F32)
        for j in range(n_group):
            counts = j < group if scan == 0 else j > group
            outside = outside + jnp.where(counts, totals[scan, c, j], 0.0)
        for j in range(GROUP):
            prefix[scan, c, j] = prefix[scan, c, j] + outside
        landing = arrived.at[scan, c, member]
        for p in near_partners:
            send(scan, 2, c, prefix.at[scan, c, p], landing, group * GROUP + p)
        arrived[scan, c, member] = prefix[scan, c, member]

    def place_states(scan, c, b, plain):
        per = HD // SLICE
        for i in range(2):
            at = slice(i * HD, (i + 1) * HD)
            s = arrived[scan, c, i * per : (i + 1) * per].reshape(HD, HD)
            s = s if plain else s + first[scan, c, i]
            pair[scan, c, b, at, at] = s.astype(BF16)

    def outer_products(scan, c, product_of, keep):
        for i in range(2):
            h = 2 * c + i
            parts = [product_of(h, b) for b in range(blocks)]
            first[scan, c, i] = parts[keep]
            per = HD // SLICE
            local[scan, c, i * per : (i + 1) * per] = (parts[0] + parts[1]).reshape(
                per, SLICE, HD
            )

    def tile(h, b):
        return slice(b * BLK, (b + 1) * BLK), slice(h * HD, (h + 1) * HD)

    def kv_product(h, b):
        return dot(k[tile(h, b)], v[tile(h, b)], TN)

    def qd_product(h, b):
        row, lane = tile(h, b)
        return dot(q_t[lane, row], dn[row, lane], NN)

    pair[...] = jnp.zeros_like(pair)
    for c in range(chunks):
        loads["k", c].wait()
        loads["v", c].wait()
        outer_products(0, c, kv_product, 0)
        if c == 0:
            pl.semaphore_wait(barrier, n_group + GROUP + n_head - 3)
        scatter(0, c)

    loads["q"].wait()

    def scores(i, _):
        h = i // blocks
        b = lax.rem(i, blocks)
        lane = pl.ds(pl.multiple_of(h * HD, HD), HD)
        r0 = pl.multiple_of(b * BLK, BLK)
        lo, hi, both = pl.ds(r0, HALF), pl.ds(r0 + HALF, HALF), pl.ds(r0, BLK)
        a0 = masked(dot(q[lo, lane], k[lo, lane], NT), lower(HALF, HALF, 0))
        a1 = masked(dot(q[hi, lane], k[both, lane], NT), lower(HALF, BLK, HALF))
        num[lo, lane] = dot(a0, v[lo, lane], NN)
        num[hi, lane] = dot(a1, v[both, lane], NN)
        t0 = masked(dot(k[lo, lane], q[both, lane], NT), upper(HALF, BLK))
        t1 = masked(dot(k[hi, lane], q[hi, lane], NT), upper(HALF, HALF))
        q_t[lane, both] = jnp.transpose(q[both, lane])
        a_t[h, b, 0:HALF, :] = t0
        a_t[h, b, HALF:BLK, HALF:BLK] = t1
        return 0

    lax.fori_loop(0, heads * blocks // 2, scores, 0)
    for c in range(chunks):
        share_totals(0, c)
    lax.fori_loop(heads * blocks // 2, heads * blocks, scores, 0)
    for c in range(chunks):
        hand_back(0, c)

    loads["g"].wait()
    loads["gain"].wait()
    gn[...] = g[...].astype(F32) * gain_ref[...]
    square = [None] * blocks
    product = [None] * blocks
    for c in range(chunks):
        wait_exchange(0, 2, c)
        for b in range(blocks):
            place_states(0, c, b, b == 0)
            for i in range(2):
                at = slice(i * HD, (i + 1) * HD)
                state[2 * c + i, b] = pair[0, c, b, at, at]
            row = slice(b * BLK, (b + 1) * BLK)
            n = num[row, cols(c)] + dot(q[row, cols(c)], pair[0, c, b], NN)
            num[row, cols(c)] = n
            sq, pr = n * n, gn[row, cols(c)] * n
            sq, pr = sq[:, :HD] + sq[:, HD:], pr[:, :HD] + pr[:, HD:]
            square[b] = sq if c == 0 else square[b] + sq
            product[b] = pr if c == 0 else product[b] + pr

    lanes = lax.broadcasted_iota(jnp.int32, (BLK, HD), 1)
    mixed = jnp.zeros((BLK, HD), F32)
    for at, x in enumerate(square + product):
        mixed = jnp.where(lanes == at, jnp.sum(x, axis=1, keepdims=True), mixed)
    stats[...] = jnp.transpose(mixed)[0 : 2 * blocks]
    all_stats[head] = stats[...]
    for p in head_partners:
        pltpu.make_async_remote_copy(
            src_ref=stats,
            dst_ref=all_stats.at[head],
            send_sem=stat_send,
            recv_sem=stat_recv,
            device_id=(seq, p),
            device_id_type=MESH,
        ).start()

    def stat_wait(sem):
        view = all_stats.at[pl.ds(0, n_head - 1)]
        pltpu.make_async_copy(view, view, sem).wait()

    stat_wait(stat_recv)
    whole = all_stats[0]
    for j in range(1, n_head):
        whole = whole + all_stats[j]
    ratio = lax.rsqrt(whole[0:blocks] / width + EPS)
    inner = whole[blocks:] / width
    weight = ratio * ratio * inner
    packed = jnp.concatenate([ratio, weight, jnp.zeros((8 - 2 * blocks, BLK), F32)], axis=0)
    turned = jnp.transpose(packed)
    ratios = [jnp.broadcast_to(turned[:, b : b + 1], (BLK, HD)) for b in range(blocks)]
    weights = [
        jnp.broadcast_to(turned[:, blocks + b : blocks + b + 1], (BLK, HD))
        for b in range(blocks)
    ]

    for c in range(chunks):
        for i in range(2):
            for b in range(blocks):
                at = tile(2 * c + i, b)
                dn[at] = (ratios[b] * (gn[at] - weights[b] * num[at])).astype(BF16)
        outer_products(1, c, qd_product, 1)
        scatter(1, c)

    for h in range(heads):
        for b in range(blocks):
            row, lane = tile(h, b)
            normed[row, lane] = (num[row, lane] * ratios[b] * gain_ref[:, lane]).astype(BF16)

    def backward(i, _):
        h = i // blocks
        b = lax.rem(i, blocks)
        lane = pl.ds(pl.multiple_of(h * HD, HD), HD)
        r0 = pl.multiple_of(b * BLK, BLK)
        lo, hi, both = pl.ds(r0, HALF), pl.ds(r0 + HALF, HALF), pl.ds(r0, BLK)
        b0 = masked(dot(dn[lo, lane], v[lo, lane], NT), lower(HALF, HALF, 0))
        b1 = masked(dot(dn[hi, lane], v[both, lane], NT), lower(HALF, BLK, HALF))
        s_bf = state[h, b]
        gq[lo, lane] = (dot(b0, k[lo, lane], NN) + dot(dn[lo, lane], s_bf, NT)).astype(BF16)
        gq[hi, lane] = (dot(b1, k[both, lane], NN) + dot(dn[hi, lane], s_bf, NT)).astype(BF16)
        t0 = masked(dot(v[lo, lane], dn[both, lane], NT), upper(HALF, BLK))
        t1 = masked(dot(v[hi, lane], dn[hi, lane], NT), upper(HALF, HALF))
        gk_part[lo, lane] = dot(t0, q[both, lane], NN)
        gk_part[hi, lane] = dot(t1, q[hi, lane], NN)
        gv_part[lo, lane] = dot(a_t[h, b, 0:HALF, :], dn[both, lane], NN)
        gv_part[hi, lane] = dot(a_t[h, b, HALF:BLK, HALF:BLK], dn[hi, lane], NN)
        return 0

    steps = heads * blocks
    lax.fori_loop(0, 3 * steps // 8, backward, 0)
    for c in range(chunks):
        share_totals(1, c)
    lax.fori_loop(3 * steps // 8, 6 * steps // 8, backward, 0)
    for c in range(chunks):
        hand_back(1, c)
    lax.fori_loop(6 * steps // 8, steps, backward, 0)

    for c in range(chunks):
        wait_exchange(1, 2, c)
        for b in range(blocks):
            place_states(1, c, b, b == blocks - 1)
            if c < chunks - 1:
                row = slice(b * BLK, (b + 1) * BLK)
                last_products(
                    row, cols(c), pair[1, c, b], v, k, gk_part, gv_part, gk, gv
                )
            else:
                later[b] = pair[1, c, b]

    for scan in range(2):
        for phase in range(3):
            for c in range(chunks):
                wait_sent(scan, phase, c)
    stat_wait(stat_send)


def finish(
    normed,
    gq,
    gk_done,
    gv_done,
    gk_part,
    gv_part,
    k,
    v,
    later,
    normed_hbm,
    gq_hbm,
    gk_hbm,
    gv_hbm,
    gk,
    gv,
    out_sem,
):
    rows, columns = k.shape
    blocks = rows // BLK
    done = slice(0, columns - 2 * HD)
    rest = slice(columns - 2 * HD, columns)
    outs = []

    def write(src, dst):
        outs.append(pltpu.make_async_copy(src, dst, out_sem.at[len(outs)]))
        outs[-1].start()

    write(normed, normed_hbm)
    write(gq, gq_hbm)
    write(gk_done.at[:, done], gk_hbm.at[:, done])
    write(gv_done.at[:, done], gv_hbm.at[:, done])
    for b in range(blocks):
        row = slice(b * BLK, (b + 1) * BLK)
        last_products(row, rest, later[b], v, k, gk_part, gv_part, gk, gv)
        write(gk.at[row, rest], gk_hbm.at[row, rest])
        write(gv.at[row, rest], gv_hbm.at[row, rest])
    for copy in outs:
        copy.wait()


def shards(queries, keys, values, gain, grad_out):
    rows, columns = queries.shape
    heads = columns // HD
    chunks = heads // 2
    blocks = rows // BLK
    n_seq, n_head = lax.axis_size("seq"), lax.axis_size("head")
    out = jax.ShapeDtypeStruct((rows, columns), BF16)
    anywhere = pl.BlockSpec(memory_space=pl.ANY)
    big = pltpu.VMEM((rows, columns), BF16)
    wide = pltpu.VMEM((rows, columns), F32)
    pieces = pltpu.VMEM((2, chunks, GROUP, SLICE, HD), F32)
    flops = heads * blocks * (12 * BLK * BLK * HD + 12 * BLK * HD * HD)
    vmem = pl.BlockSpec(memory_space=pltpu.VMEM)
    hbm = [
        pltpu.with_memory_space_constraint(x, pltpu.HBM)
        for x in (queries, keys, values, gain.reshape(1, columns), grad_out)
    ]
    kept = (
        pltpu.VMEM((rows, columns), BF16),
        pltpu.VMEM((rows, columns), BF16),
        pltpu.VMEM((rows, columns), BF16),
        pltpu.VMEM((rows, columns), BF16),
        pltpu.VMEM((rows, columns), F32),
        pltpu.VMEM((rows, columns), F32),
        pltpu.VMEM((rows, columns), BF16),
        pltpu.VMEM((rows, columns), BF16),
        pltpu.VMEM((blocks, 2 * HD, 2 * HD), BF16),
    )
    held = pl.pallas_call(
        functools.partial(kernel, n_seq, n_head, columns * n_head),
        out_shape=kept,
        in_specs=[anywhere] * 5,
        out_specs=(vmem,) * len(kept),
        scratch_shapes=[
            big,
            big,
            pltpu.VMEM((1, columns), F32),
            wide,
            pltpu.VMEM((columns, rows), BF16),
            wide,
            big,
            pltpu.VMEM((2, chunks, 2, HD, HD), F32),
            pieces,
            pltpu.VMEM((heads, blocks, HD, HD), BF16),
            pltpu.VMEM((2, chunks, blocks, 2 * HD, 2 * HD), BF16),
            pltpu.VMEM((heads, blocks, BLK, BLK), BF16),
            pieces,
            pieces,
            pieces,
            pltpu.VMEM((2, chunks, n_seq // GROUP, SLICE, HD), F32),
            pltpu.VMEM((2 * blocks, BLK), F32),
            pltpu.VMEM((n_head, 2 * blocks, BLK), F32),
            pltpu.SemaphoreType.DMA((2 * chunks + 3,)),
            pltpu.SemaphoreType.DMA((6 * chunks,)),
            pltpu.SemaphoreType.DMA((6 * chunks,)),
            pltpu.SemaphoreType.DMA,
            pltpu.SemaphoreType.DMA,
        ],
        compiler_params=pltpu.CompilerParams(
            collective_id=0, has_side_effects=True, vmem_limit_bytes=32 << 20
        ),
        cost_estimate=pl.CostEstimate(
            flops=flops, bytes_accessed=4 * rows * columns * 2, transcendentals=0
        ),
    )(*hbm)
    return pl.pallas_call(
        finish,
        out_shape=(out, out, out, out),
        in_specs=[vmem] * len(kept),
        out_specs=(anywhere,) * 4,
        scratch_shapes=[big, big, pltpu.SemaphoreType.DMA((4 + 2 * blocks,))],
        compiler_params=pltpu.CompilerParams(vmem_limit_bytes=24 << 20),
        cost_estimate=pl.CostEstimate(
            flops=heads * blocks * 4 * BLK * HD * HD,
            bytes_accessed=4 * rows * columns * 2,
            transcendentals=0,
        ),
    )(*held)


def solution(mesh):
    spec = P("seq", "head")
    return jax.shard_map(
        shards,
        mesh=mesh,
        in_specs=(spec, spec, spec, P("head"), spec),
        out_specs=(spec, spec, spec, spec),
        check_vma=False,
    )
```

```python
import functools

import jax
import jax.numpy as jnp
from jax import lax
from jax.experimental import pallas as pl
from jax.experimental.pallas import tpu as pltpu
from jax.sharding import PartitionSpec as P

HD = 128
BLK = 512
HALF = BLK // 2
EPS = 1e-06
GROUP = 8
SLICE = HD // GROUP
X = 4
CORES = 2
MESH = pl.DeviceIdType.MESH

F32 = jnp.float32
BF16 = jnp.bfloat16

NN = (((1,), (0,)), ((), ()))
NT = (((1,), (1,)), ((), ()))
TN = (((0,), (0,)), ((), ()))


def far_first(me, n, inner):
    outer = n // inner
    major, minor = me // inner, lax.rem(me, inner)

    def hops(step):
        return min(step[0], outer - step[0]) + min(step[1], inner - step[1])

    steps = [(i, j) for i in range(outer) for j in range(inner) if i + j]
    return [
        lax.rem(major + i, outer) * inner + lax.rem(minor + j, inner)
        for i, j in sorted(steps, key=hops, reverse=True)
    ]


def dot(a, b, dims):
    return lax.dot_general(a, b, dims, preferred_element_type=F32)


def lower(rows, columns, offset):
    s = lax.broadcasted_iota(jnp.int32, (rows, columns), 0) + offset
    t = lax.broadcasted_iota(jnp.int32, (rows, columns), 1)
    return t <= s


def upper(rows, columns):
    t = lax.broadcasted_iota(jnp.int32, (rows, columns), 0)
    s = lax.broadcasted_iota(jnp.int32, (rows, columns), 1)
    return t <= s


def masked(scores, mask):
    return jnp.where(mask, scores, 0.0).astype(BF16)


def last_products(row, lane, r, v, k, gk_part, gv_part, gk, gv):
    gk[row, lane] = (gk_part[row, lane] + dot(v[row, lane], r, NT)).astype(BF16)
    gv[row, lane] = (gv_part[row, lane] + dot(k[row, lane], r, NN)).astype(BF16)


def kernel(
    n_seq,
    n_head,
    width,
    q_hbm,
    k_hbm,
    v_hbm,
    gain_hbm,
    g_hbm,
    normed,
    gq,
    gk,
    gv,
    gk_part,
    gv_part,
    k,
    v,
    later,
    q,
    g,
    gain_ref,
    gn,
    q_t,
    num,
    dn,
    first,
    local,
    state,
    pair,
    a_t,
    gathered,
    prefix,
    arrived,
    here,
    totals,
    stats,
    all_stats,
    in_sem,
    send_sem,
    recv_sem,
    far_send_sem,
    far_recv_sem,
    entered,
    stat_send,
    stat_recv,
):
    rows, columns = q.shape
    heads = columns // HD
    chunks = heads // 2
    blocks = rows // BLK
    seq = lax.axis_index("seq")
    head = lax.axis_index("head")
    n_group = n_seq // GROUP
    group, member = seq // GROUP, lax.rem(seq, GROUP)
    near_partners = far_first(member, GROUP, X)
    far_partners = far_first(group, n_group, 1)
    head_partners = far_first(head, n_head, CORES)

    def cols(c):
        return slice(c * 2 * HD, (c + 1) * 2 * HD)

    barrier = pltpu.get_barrier_semaphore()
    for p in far_partners:

        @pl.when(p > group)
        def _():
            to = (p * GROUP + member, head)
            pl.semaphore_signal(barrier, inc=1, device_id=to, device_id_type=MESH)

    for p in near_partners:
        to = (group * GROUP + p, head)
        pl.semaphore_signal(barrier, inc=1, device_id=to, device_id_type=MESH)
    for p in head_partners:
        pl.semaphore_signal(barrier, inc=1, device_id=(seq, p), device_id_type=MESH)

    loads = {}
    for c in range(chunks):
        for i, (name, src, dst) in enumerate((("k", k_hbm, k), ("v", v_hbm, v))):
            loads[name, c] = pltpu.make_async_copy(
                src.at[:, cols(c)], dst.at[:, cols(c)], in_sem.at[2 * c + i]
            )
            loads[name, c].start()
    for i, (name, src, dst) in enumerate(
        (("q", q_hbm, q), ("g", g_hbm, g), ("gain", gain_hbm, gain_ref))
    ):
        loads[name] = pltpu.make_async_copy(src, dst, in_sem.at[2 * chunks + i])
        loads[name].start()

    def near(scan, phase, h):
        return (scan * 2 + phase) * heads + h

    def send_near(scan, phase, h, source, landing):
        for p in near_partners:
            pltpu.make_async_remote_copy(
                src_ref=source.at[scan, h, p],
                dst_ref=landing.at[scan, h, member],
                send_sem=send_sem.at[near(scan, phase, h)],
                recv_sem=recv_sem.at[near(scan, phase, h)],
                device_id=(group * GROUP + p, head),
                device_id_type=MESH,
            ).start()
        landing[scan, h, member] = source[scan, h, member]

    def wait_near(sem, scan, phase, h):
        view = gathered.at[scan, h, pl.ds(0, GROUP - 1)]
        pltpu.make_async_copy(view, view, sem.at[near(scan, phase, h)]).wait()

    def ahead(scan, p):
        return p > group if scan == 0 else p < group

    def far_send(scan, h, i):
        p = far_partners[i]
        return pltpu.make_async_remote_copy(
            src_ref=here.at[scan, h],
            dst_ref=totals.at[scan, h, group],
            send_sem=far_send_sem.at[(scan * heads + h) * (n_group - 1) + i],
            recv_sem=far_recv_sem.at[(scan * heads + h) * n_group + group],
            device_id=(p * GROUP + member, head),
            device_id_type=MESH,
        )

    def scatter(scan, h):
        send_near(scan, 0, h, local, gathered)

    def share_totals(scan, h):
        wait_near(recv_sem, scan, 0, h)
        sum_here = jnp.zeros((SLICE, HD), F32)
        for j in range(GROUP) if scan == 0 else range(GROUP - 1, -1, -1):
            prefix[scan, h, j] = sum_here
            sum_here = sum_here + gathered[scan, h, j]
        here[scan, h] = sum_here
        if scan == 0 and h == 0:

            @pl.when(group < n_group - 1)
            def _():
                pl.semaphore_wait(entered, n_group - 1 - group)

        for i, p in enumerate(far_partners):

            @pl.when(ahead(scan, p))
            def _():
                far_send(scan, h, i).start()

    def hand_back(scan, h):
        outside = jnp.zeros((SLICE, HD), F32)
        for j in range(n_group):

            @pl.when(group > j if scan == 0 else group < j)
            def _():
                view = totals.at[scan, h, j]
                sem = far_recv_sem.at[(scan * heads + h) * n_group + j]
                pltpu.make_async_copy(view, view, sem).wait()

        for j in range(n_group):
            outside = outside + totals[scan, h, j]
        for j in range(GROUP):
            prefix[scan, h, j] = prefix[scan, h, j] + outside
        send_near(scan, 1, h, prefix, arrived)

    def wait_sent(scan, h):
        for phase in range(2):
            wait_near(send_sem, scan, phase, h)
        for i, p in enumerate(far_partners):

            @pl.when(ahead(scan, p))
            def _():
                far_send(scan, h, i).wait_send()

    def place_states(scan, c, b, plain):
        for i in range(2):
            at = slice(i * HD, (i + 1) * HD)
            s = arrived[scan, 2 * c + i].reshape(HD, HD)
            s = s if plain else s + first[scan, 2 * c + i]
            pair[scan, c, b, at, at] = s.astype(BF16)

    def outer_products(scan, h, product_of, keep):
        parts = [product_of(h, b) for b in range(blocks)]
        first[scan, h] = parts[keep]
        local[scan, h] = sum(parts[1:], parts[0]).reshape(GROUP, SLICE, HD)

    def tile(h, b):
        return slice(b * BLK, (b + 1) * BLK), slice(h * HD, (h + 1) * HD)

    def kv_product(h, b):
        return dot(k[tile(h, b)], v[tile(h, b)], TN)

    def qd_product(h, b):
        row, lane = tile(h, b)
        return dot(q_t[lane, row], dn[row, lane], NN)

    pair[...] = jnp.zeros_like(pair)
    totals[...] = jnp.zeros_like(totals)
    for c in range(chunks):
        loads["k", c].wait()
        loads["v", c].wait()
        for i in range(2):
            outer_products(0, 2 * c + i, kv_product, 0)
    pl.semaphore_wait(barrier, GROUP + n_head - 2 + group)
    for p in far_partners:

        @pl.when(p < group)
        def _():
            to = (p * GROUP + member, head)
            pl.semaphore_signal(entered, inc=1, device_id=to, device_id_type=MESH)

    for h in range(heads):
        scatter(0, h)

    loads["q"].wait()

    def scores(i, _):
        h = i // blocks
        b = lax.rem(i, blocks)
        lane = pl.ds(pl.multiple_of(h * HD, HD), HD)
        r0 = pl.multiple_of(b * BLK, BLK)
        lo, hi, both = pl.ds(r0, HALF), pl.ds(r0 + HALF, HALF), pl.ds(r0, BLK)
        a0 = masked(dot(q[lo, lane], k[lo, lane], NT), lower(HALF, HALF, 0))
        a1 = masked(dot(q[hi, lane], k[both, lane], NT), lower(HALF, BLK, HALF))
        num[lo, lane] = dot(a0, v[lo, lane], NN)
        num[hi, lane] = dot(a1, v[both, lane], NN)
        t0 = masked(dot(k[lo, lane], q[both, lane], NT), upper(HALF, BLK))
        t1 = masked(dot(k[hi, lane], q[hi, lane], NT), upper(HALF, HALF))
        q_t[lane, both] = jnp.transpose(q[both, lane])
        a_t[h, b, 0:HALF, :] = t0
        a_t[h, b, HALF:BLK, HALF:BLK] = t1
        return 0

    lax.fori_loop(0, heads * blocks // 2, scores, 0)
    for h in range(heads):
        share_totals(0, h)
    lax.fori_loop(heads * blocks // 2, heads * blocks, scores, 0)
    for h in range(heads):
        hand_back(0, h)

    loads["g"].wait()
    loads["gain"].wait()
    gn[...] = g[...].astype(F32) * gain_ref[...]
    square = [None] * blocks
    product = [None] * blocks
    for c in range(chunks):
        for i in range(2):
            wait_near(recv_sem, 0, 1, 2 * c + i)
        for b in range(blocks):
            place_states(0, c, b, b == 0)
            for i in range(2):
                at = slice(i * HD, (i + 1) * HD)
                state[2 * c + i, b] = pair[0, c, b, at, at]
            row = slice(b * BLK, (b + 1) * BLK)
            n = num[row, cols(c)] + dot(q[row, cols(c)], pair[0, c, b], NN)
            num[row, cols(c)] = n
            sq, pr = n * n, gn[row, cols(c)] * n
            sq, pr = sq[:, :HD] + sq[:, HD:], pr[:, :HD] + pr[:, HD:]
            square[b] = sq if c == 0 else square[b] + sq
            product[b] = pr if c == 0 else product[b] + pr

    lanes = lax.broadcasted_iota(jnp.int32, (BLK, HD), 1)
    mixed = jnp.zeros((BLK, HD), F32)
    for at, x in enumerate(square + product):
        mixed = jnp.where(lanes == at, jnp.sum(x, axis=1, keepdims=True), mixed)
    stats[...] = jnp.transpose(mixed)[0 : 2 * blocks]
    all_stats[head] = stats[...]
    for p in head_partners:
        pltpu.make_async_remote_copy(
            src_ref=stats,
            dst_ref=all_stats.at[head],
            send_sem=stat_send,
            recv_sem=stat_recv,
            device_id=(seq, p),
            device_id_type=MESH,
        ).start()

    def stat_wait(sem):
        view = all_stats.at[pl.ds(0, n_head - 1)]
        pltpu.make_async_copy(view, view, sem).wait()

    stat_wait(stat_recv)
    whole = all_stats[0]
    for j in range(1, n_head):
        whole = whole + all_stats[j]
    ratio = lax.rsqrt(whole[0:blocks] / width + EPS)
    inner = whole[blocks:] / width
    weight = ratio * ratio * inner
    packed = jnp.concatenate([ratio, weight, jnp.zeros((8 - 2 * blocks, BLK), F32)], axis=0)
    turned = jnp.transpose(packed)
    ratios = [jnp.broadcast_to(turned[:, b : b + 1], (BLK, HD)) for b in range(blocks)]
    weights = [
        jnp.broadcast_to(turned[:, blocks + b : blocks + b + 1], (BLK, HD))
        for b in range(blocks)
    ]

    for h in range(heads):
        for b in range(blocks):
            at = tile(h, b)
            dn[at] = (ratios[b] * (gn[at] - weights[b] * num[at])).astype(BF16)
        outer_products(1, h, qd_product, 1)
        scatter(1, h)

    for h in range(heads):
        for b in range(blocks):
            row, lane = tile(h, b)
            normed[row, lane] = (num[row, lane] * ratios[b] * gain_ref[:, lane]).astype(BF16)

    def backward(i, _):
        h = i // blocks
        b = lax.rem(i, blocks)
        lane = pl.ds(pl.multiple_of(h * HD, HD), HD)
        r0 = pl.multiple_of(b * BLK, BLK)
        lo, hi, both = pl.ds(r0, HALF), pl.ds(r0 + HALF, HALF), pl.ds(r0, BLK)
        b0 = masked(dot(dn[lo, lane], v[lo, lane], NT), lower(HALF, HALF, 0))
        b1 = masked(dot(dn[hi, lane], v[both, lane], NT), lower(HALF, BLK, HALF))
        s_bf = state[h, b]
        gq[lo, lane] = (dot(b0, k[lo, lane], NN) + dot(dn[lo, lane], s_bf, NT)).astype(BF16)
        gq[hi, lane] = (dot(b1, k[both, lane], NN) + dot(dn[hi, lane], s_bf, NT)).astype(BF16)
        t0 = masked(dot(v[lo, lane], dn[both, lane], NT), upper(HALF, BLK))
        t1 = masked(dot(v[hi, lane], dn[hi, lane], NT), upper(HALF, HALF))
        gk_part[lo, lane] = dot(t0, q[both, lane], NN)
        gk_part[hi, lane] = dot(t1, q[hi, lane], NN)
        gv_part[lo, lane] = dot(a_t[h, b, 0:HALF, :], dn[both, lane], NN)
        gv_part[hi, lane] = dot(a_t[h, b, HALF:BLK, HALF:BLK], dn[hi, lane], NN)
        return 0

    steps = heads * blocks
    lax.fori_loop(0, 3 * steps // 8, backward, 0)
    for h in range(heads):
        share_totals(1, h)
    lax.fori_loop(3 * steps // 8, 6 * steps // 8, backward, 0)
    for h in range(heads):
        hand_back(1, h)
    lax.fori_loop(6 * steps // 8, steps, backward, 0)

    for c in range(chunks):
        for i in range(2):
            wait_near(recv_sem, 1, 1, 2 * c + i)
        for b in range(blocks):
            place_states(1, c, b, b == blocks - 1)
            if c < chunks - 1:
                row = slice(b * BLK, (b + 1) * BLK)
                last_products(
                    row, cols(c), pair[1, c, b], v, k, gk_part, gv_part, gk, gv
                )
            else:
                later[b] = pair[1, c, b]

    for scan in range(2):
        for h in range(heads):
            wait_sent(scan, h)
    stat_wait(stat_send)


def finish(
    normed,
    gq,
    gk_done,
    gv_done,
    gk_part,
    gv_part,
    k,
    v,
    later,
    normed_hbm,
    gq_hbm,
    gk_hbm,
    gv_hbm,
    gk,
    gv,
    out_sem,
):
    rows, columns = k.shape
    blocks = rows // BLK
    done = slice(0, columns - 2 * HD)
    rest = slice(columns - 2 * HD, columns)
    outs = []

    def write(src, dst):
        outs.append(pltpu.make_async_copy(src, dst, out_sem.at[len(outs)]))
        outs[-1].start()

    write(normed, normed_hbm)
    write(gq, gq_hbm)
    write(gk_done.at[:, done], gk_hbm.at[:, done])
    write(gv_done.at[:, done], gv_hbm.at[:, done])
    for b in range(blocks):
        row = slice(b * BLK, (b + 1) * BLK)
        last_products(row, rest, later[b], v, k, gk_part, gv_part, gk, gv)
        write(gk.at[row, rest], gk_hbm.at[row, rest])
        write(gv.at[row, rest], gv_hbm.at[row, rest])
    for copy in outs:
        copy.wait()


def shards(queries, keys, values, gain, grad_out):
    rows, columns = queries.shape
    heads = columns // HD
    chunks = heads // 2
    blocks = rows // BLK
    n_seq, n_head = lax.axis_size("seq"), lax.axis_size("head")
    out = jax.ShapeDtypeStruct((rows, columns), BF16)
    anywhere = pl.BlockSpec(memory_space=pl.ANY)
    big = pltpu.VMEM((rows, columns), BF16)
    wide = pltpu.VMEM((rows, columns), F32)
    pieces = pltpu.VMEM((2, heads, GROUP, SLICE, HD), F32)
    flops = heads * blocks * (12 * BLK * BLK * HD + 12 * BLK * HD * HD)
    vmem = pl.BlockSpec(memory_space=pltpu.VMEM)
    hbm = [
        pltpu.with_memory_space_constraint(x, pltpu.HBM)
        for x in (queries, keys, values, gain.reshape(1, columns), grad_out)
    ]
    kept = (
        pltpu.VMEM((rows, columns), BF16),
        pltpu.VMEM((rows, columns), BF16),
        pltpu.VMEM((rows, columns), BF16),
        pltpu.VMEM((rows, columns), BF16),
        pltpu.VMEM((rows, columns), F32),
        pltpu.VMEM((rows, columns), F32),
        pltpu.VMEM((rows, columns), BF16),
        pltpu.VMEM((rows, columns), BF16),
        pltpu.VMEM((blocks, 2 * HD, 2 * HD), BF16),
    )
    held = pl.pallas_call(
        functools.partial(kernel, n_seq, n_head, columns * n_head),
        out_shape=kept,
        in_specs=[anywhere] * 5,
        out_specs=(vmem,) * len(kept),
        scratch_shapes=[
            big,
            big,
            pltpu.VMEM((1, columns), F32),
            wide,
            pltpu.VMEM((columns, rows), BF16),
            wide,
            big,
            pltpu.VMEM((2, heads, HD, HD), F32),
            pieces,
            pltpu.VMEM((heads, blocks, HD, HD), BF16),
            pltpu.VMEM((2, chunks, blocks, 2 * HD, 2 * HD), BF16),
            pltpu.VMEM((heads, blocks, BLK, BLK), BF16),
            pieces,
            pieces,
            pieces,
            pltpu.VMEM((2, heads, SLICE, HD), F32),
            pltpu.VMEM((2, heads, n_seq // GROUP, SLICE, HD), F32),
            pltpu.VMEM((2 * blocks, BLK), F32),
            pltpu.VMEM((n_head, 2 * blocks, BLK), F32),
            pltpu.SemaphoreType.DMA((2 * chunks + 3,)),
            pltpu.SemaphoreType.DMA((4 * heads,)),
            pltpu.SemaphoreType.DMA((4 * heads,)),
            pltpu.SemaphoreType.DMA((2 * heads * (n_seq // GROUP - 1),)),
            pltpu.SemaphoreType.DMA((2 * heads * (n_seq // GROUP),)),
            pltpu.SemaphoreType.REGULAR,
            pltpu.SemaphoreType.DMA,
            pltpu.SemaphoreType.DMA,
        ],
        compiler_params=pltpu.CompilerParams(
            collective_id=0, has_side_effects=True, vmem_limit_bytes=32 << 20
        ),
        cost_estimate=pl.CostEstimate(
            flops=flops, bytes_accessed=4 * rows * columns * 2, transcendentals=0
        ),
    )(*hbm)
    return pl.pallas_call(
        finish,
        out_shape=(out, out, out, out),
        in_specs=[vmem] * len(kept),
        out_specs=(anywhere,) * 4,
        scratch_shapes=[big, big, pltpu.SemaphoreType.DMA((4 + 2 * blocks,))],
        compiler_params=pltpu.CompilerParams(vmem_limit_bytes=24 << 20),
        cost_estimate=pl.CostEstimate(
            flops=heads * blocks * 4 * BLK * HD * HD,
            bytes_accessed=4 * rows * columns * 2,
            transcendentals=0,
        ),
    )(*held)


def solution(mesh):
    spec = P("seq", "head")
    return jax.shard_map(
        shards,
        mesh=mesh,
        in_specs=(spec, spec, spec, P("head"), spec),
        out_specs=(spec, spec, spec, spec),
        check_vma=False,
    )
```

```python
import functools

import jax
import jax.numpy as jnp
from jax import lax
from jax.experimental import pallas as pl
from jax.experimental.pallas import tpu as pltpu
from jax.sharding import PartitionSpec as P

HD = 128
BLK = 512
HALF = BLK // 2
EPS = 1e-06
GROUP = 8
SLICE = HD // GROUP
X = 4
CORES = 2
MESH = pl.DeviceIdType.MESH

F32 = jnp.float32
BF16 = jnp.bfloat16

NN = (((1,), (0,)), ((), ()))
NT = (((1,), (1,)), ((), ()))
TN = (((0,), (0,)), ((), ()))


def far_first(me, n, inner):
    outer = n // inner
    major, minor = me // inner, lax.rem(me, inner)

    def hops(step):
        return min(step[0], outer - step[0]) + min(step[1], inner - step[1])

    steps = [(i, j) for i in range(outer) for j in range(inner) if i + j]
    return [
        lax.rem(major + i, outer) * inner + lax.rem(minor + j, inner)
        for i, j in sorted(steps, key=hops, reverse=True)
    ]


def dot(a, b, dims):
    return lax.dot_general(a, b, dims, preferred_element_type=F32)


def lower(rows, columns, offset):
    s = lax.broadcasted_iota(jnp.int32, (rows, columns), 0) + offset
    t = lax.broadcasted_iota(jnp.int32, (rows, columns), 1)
    return t <= s


def upper(rows, columns):
    t = lax.broadcasted_iota(jnp.int32, (rows, columns), 0)
    s = lax.broadcasted_iota(jnp.int32, (rows, columns), 1)
    return t <= s


def masked(scores, mask):
    return jnp.where(mask, scores, 0.0).astype(BF16)


def last_products(row, lane, r, v, k, gk_part, gv_part, gk, gv):
    gk[row, lane] = (gk_part[row, lane] + dot(v[row, lane], r, NT)).astype(BF16)
    gv[row, lane] = (gv_part[row, lane] + dot(k[row, lane], r, NN)).astype(BF16)


def kernel(
    n_seq,
    n_head,
    width,
    q_hbm,
    k_hbm,
    v_hbm,
    gain_hbm,
    g_hbm,
    normed,
    gq,
    gk,
    gv,
    gk_part,
    gv_part,
    k,
    v,
    later,
    q,
    g,
    gain_ref,
    gn,
    q_t,
    num,
    dn,
    first,
    local,
    state,
    pair,
    a_t,
    gathered,
    prefix,
    arrived,
    here,
    totals,
    stats,
    all_stats,
    in_sem,
    send_sem,
    recv_sem,
    far_send_sem,
    far_recv_sem,
    entered,
    stat_send,
    stat_recv,
):
    rows, columns = q.shape
    heads = columns // HD
    chunks = heads // 2
    blocks = rows // BLK
    seq = lax.axis_index("seq")
    head = lax.axis_index("head")
    n_group = n_seq // GROUP
    group, member = seq // GROUP, lax.rem(seq, GROUP)
    near_partners = far_first(member, GROUP, X)
    far_partners = far_first(group, n_group, 1)
    head_partners = far_first(head, n_head, CORES)

    def cols(c):
        return slice(c * 2 * HD, (c + 1) * 2 * HD)

    barrier = pltpu.get_barrier_semaphore()
    for p in far_partners:

        @pl.when(p > group)
        def _():
            to = (p * GROUP + member, head)
            pl.semaphore_signal(barrier, inc=1, device_id=to, device_id_type=MESH)

    for p in near_partners:
        to = (group * GROUP + p, head)
        pl.semaphore_signal(barrier, inc=1, device_id=to, device_id_type=MESH)
    for p in head_partners:
        pl.semaphore_signal(barrier, inc=1, device_id=(seq, p), device_id_type=MESH)

    loads = {}
    for c in range(chunks):
        for i, (name, src, dst) in enumerate((("k", k_hbm, k), ("v", v_hbm, v))):
            loads[name, c] = pltpu.make_async_copy(
                src.at[:, cols(c)], dst.at[:, cols(c)], in_sem.at[2 * c + i]
            )
            loads[name, c].start()
    for i, (name, src, dst) in enumerate(
        (("q", q_hbm, q), ("g", g_hbm, g), ("gain", gain_hbm, gain_ref))
    ):
        loads[name] = pltpu.make_async_copy(src, dst, in_sem.at[2 * chunks + i])
        loads[name].start()

    def near(scan, phase, h):
        return (scan * 2 + phase) * heads + h

    def send_near(scan, phase, h, source, landing):
        for p in near_partners:
            pltpu.make_async_remote_copy(
                src_ref=source.at[scan, h, p],
                dst_ref=landing.at[scan, h, member],
                send_sem=send_sem.at[near(scan, phase, h)],
                recv_sem=recv_sem.at[near(scan, phase, h)],
                device_id=(group * GROUP + p, head),
                device_id_type=MESH,
            ).start()
        landing[scan, h, member] = source[scan, h, member]

    def wait_near(sem, scan, phase, h):
        view = gathered.at[scan, h, pl.ds(0, GROUP - 1)]
        pltpu.make_async_copy(view, view, sem.at[near(scan, phase, h)]).wait()

    def ahead(scan, p):
        return p > group if scan == 0 else p < group

    def far_send(scan, h, i):
        p = far_partners[i]
        return pltpu.make_async_remote_copy(
            src_ref=here.at[scan, h],
            dst_ref=totals.at[scan, h, group],
            send_sem=far_send_sem.at[(scan * heads + h) * (n_group - 1) + i],
            recv_sem=far_recv_sem.at[(scan * heads + h) * n_group + group],
            device_id=(p * GROUP + member, head),
            device_id_type=MESH,
        )

    def scatter(scan, h):
        send_near(scan, 0, h, local, gathered)

    def share_totals(scan, h):
        wait_near(recv_sem, scan, 0, h)
        sum_here = jnp.zeros((SLICE, HD), F32)
        for j in range(GROUP) if scan == 0 else range(GROUP - 1, -1, -1):
            prefix[scan, h, j] = sum_here
            sum_here = sum_here + gathered[scan, h, j]
        here[scan, h] = sum_here
        if scan == 0 and h == 0:

            @pl.when(group < n_group - 1)
            def _():
                pl.semaphore_wait(entered, n_group - 1 - group)

        for i, p in enumerate(far_partners):

            @pl.when(ahead(scan, p))
            def _():
                far_send(scan, h, i).start()

    def hand_back(scan, h):
        outside = jnp.zeros((SLICE, HD), F32)
        for j in range(n_group):

            @pl.when(group > j if scan == 0 else group < j)
            def _():
                view = totals.at[scan, h, j]
                sem = far_recv_sem.at[(scan * heads + h) * n_group + j]
                pltpu.make_async_copy(view, view, sem).wait()

        for j in range(n_group):
            outside = outside + totals[scan, h, j]
        for j in range(GROUP):
            prefix[scan, h, j] = prefix[scan, h, j] + outside
        send_near(scan, 1, h, prefix, arrived)

    def wait_sent(scan, h):
        for phase in range(2):
            wait_near(send_sem, scan, phase, h)
        for i, p in enumerate(far_partners):

            @pl.when(ahead(scan, p))
            def _():
                far_send(scan, h, i).wait_send()

    def place_states(scan, c, b, plain):
        for i in range(2):
            at = slice(i * HD, (i + 1) * HD)
            s = arrived[scan, 2 * c + i].reshape(HD, HD)
            s = s if plain else s + first[scan, 2 * c + i]
            pair[scan, c, b, at, at] = s.astype(BF16)

    def outer_products(scan, h, product_of, keep):
        parts = [product_of(h, b) for b in range(blocks)]
        first[scan, h] = parts[keep]
        local[scan, h] = sum(parts[1:], parts[0]).reshape(GROUP, SLICE, HD)

    def tile(h, b):
        return slice(b * BLK, (b + 1) * BLK), slice(h * HD, (h + 1) * HD)

    def kv_product(h, b):
        return dot(k[tile(h, b)], v[tile(h, b)], TN)

    def qd_product(h, b):
        row, lane = tile(h, b)
        return dot(q_t[lane, row], dn[row, lane], NN)

    pair[...] = jnp.zeros_like(pair)
    totals[...] = jnp.zeros_like(totals)
    for c in range(chunks):
        loads["k", c].wait()
        loads["v", c].wait()
        for i in range(2):
            outer_products(0, 2 * c + i, kv_product, 0)
    pl.semaphore_wait(barrier, GROUP + n_head - 2 + group)
    for p in far_partners:

        @pl.when(p < group)
        def _():
            to = (p * GROUP + member, head)
            pl.semaphore_signal(entered, inc=1, device_id=to, device_id_type=MESH)

    for h in range(heads):
        scatter(0, h)

    loads["q"].wait()

    def scores(i, _):
        h = i // blocks
        b = lax.rem(i, blocks)
        lane = pl.ds(pl.multiple_of(h * HD, HD), HD)
        r0 = pl.multiple_of(b * BLK, BLK)
        lo, hi, both = pl.ds(r0, HALF), pl.ds(r0 + HALF, HALF), pl.ds(r0, BLK)
        a0 = masked(dot(q[lo, lane], k[lo, lane], NT), lower(HALF, HALF, 0))
        a1 = masked(dot(q[hi, lane], k[both, lane], NT), lower(HALF, BLK, HALF))
        num[lo, lane] = dot(a0, v[lo, lane], NN)
        num[hi, lane] = dot(a1, v[both, lane], NN)
        t0 = masked(dot(k[lo, lane], q[both, lane], NT), upper(HALF, BLK))
        t1 = masked(dot(k[hi, lane], q[hi, lane], NT), upper(HALF, HALF))
        q_t[lane, both] = jnp.transpose(q[both, lane])
        a_t[h, b, 0:HALF, :] = t0
        a_t[h, b, HALF:BLK, HALF:BLK] = t1
        return 0

    lax.fori_loop(0, heads * blocks // 2, scores, 0)
    for h in range(heads):
        share_totals(0, h)
    lax.fori_loop(heads * blocks // 2, heads * blocks, scores, 0)
    for h in range(heads):
        hand_back(0, h)

    loads["g"].wait()
    loads["gain"].wait()
    gn[...] = g[...].astype(F32) * gain_ref[...]
    square = [None] * blocks
    product = [None] * blocks
    for c in range(chunks):
        for i in range(2):
            wait_near(recv_sem, 0, 1, 2 * c + i)
        for b in range(blocks):
            place_states(0, c, b, b == 0)
            for i in range(2):
                at = slice(i * HD, (i + 1) * HD)
                state[2 * c + i, b] = pair[0, c, b, at, at]
            row = slice(b * BLK, (b + 1) * BLK)
            n = num[row, cols(c)] + dot(q[row, cols(c)], pair[0, c, b], NN)
            num[row, cols(c)] = n
            sq, pr = n * n, gn[row, cols(c)] * n
            sq, pr = sq[:, :HD] + sq[:, HD:], pr[:, :HD] + pr[:, HD:]
            square[b] = sq if c == 0 else square[b] + sq
            product[b] = pr if c == 0 else product[b] + pr

    lanes = lax.broadcasted_iota(jnp.int32, (BLK, HD), 1)
    mixed = jnp.zeros((BLK, HD), F32)
    for at, x in enumerate(square + product):
        mixed = jnp.where(lanes == at, jnp.sum(x, axis=1, keepdims=True), mixed)
    stats[...] = jnp.transpose(mixed)[0 : 2 * blocks]
    all_stats[head] = stats[...]
    for p in head_partners:
        pltpu.make_async_remote_copy(
            src_ref=stats,
            dst_ref=all_stats.at[head],
            send_sem=stat_send,
            recv_sem=stat_recv,
            device_id=(seq, p),
            device_id_type=MESH,
        ).start()

    def stat_wait(sem):
        view = all_stats.at[pl.ds(0, n_head - 1)]
        pltpu.make_async_copy(view, view, sem).wait()

    stat_wait(stat_recv)
    whole = all_stats[0]
    for j in range(1, n_head):
        whole = whole + all_stats[j]
    ratio = lax.rsqrt(whole[0:blocks] / width + EPS)
    inner = whole[blocks:] / width
    weight = ratio * ratio * inner
    packed = jnp.concatenate([ratio, weight, jnp.zeros((8 - 2 * blocks, BLK), F32)], axis=0)
    turned = jnp.transpose(packed)
    ratios = [jnp.broadcast_to(turned[:, b : b + 1], (BLK, HD)) for b in range(blocks)]
    weights = [
        jnp.broadcast_to(turned[:, blocks + b : blocks + b + 1], (BLK, HD))
        for b in range(blocks)
    ]

    for h in range(heads):
        for b in range(blocks):
            at = tile(h, b)
            dn[at] = (ratios[b] * (gn[at] - weights[b] * num[at])).astype(BF16)
        outer_products(1, h, qd_product, 1)
        scatter(1, h)

    for h in range(heads):
        for b in range(blocks):
            row, lane = tile(h, b)
            normed[row, lane] = (num[row, lane] * ratios[b] * gain_ref[:, lane]).astype(BF16)

    def backward(i, _):
        h = i // blocks
        b = lax.rem(i, blocks)
        lane = pl.ds(pl.multiple_of(h * HD, HD), HD)
        r0 = pl.multiple_of(b * BLK, BLK)
        lo, hi, both = pl.ds(r0, HALF), pl.ds(r0 + HALF, HALF), pl.ds(r0, BLK)
        b0 = masked(dot(dn[lo, lane], v[lo, lane], NT), lower(HALF, HALF, 0))
        b1 = masked(dot(dn[hi, lane], v[both, lane], NT), lower(HALF, BLK, HALF))
        s_bf = state[h, b]
        gq[lo, lane] = (dot(b0, k[lo, lane], NN) + dot(dn[lo, lane], s_bf, NT)).astype(BF16)
        gq[hi, lane] = (dot(b1, k[both, lane], NN) + dot(dn[hi, lane], s_bf, NT)).astype(BF16)
        t0 = masked(dot(v[lo, lane], dn[both, lane], NT), upper(HALF, BLK))
        t1 = masked(dot(v[hi, lane], dn[hi, lane], NT), upper(HALF, HALF))
        gk_part[lo, lane] = dot(t0, q[both, lane], NN)
        gk_part[hi, lane] = dot(t1, q[hi, lane], NN)
        gv_part[lo, lane] = dot(a_t[h, b, 0:HALF, :], dn[both, lane], NN)
        gv_part[hi, lane] = dot(a_t[h, b, HALF:BLK, HALF:BLK], dn[hi, lane], NN)
        return 0

    steps = heads * blocks
    lax.fori_loop(0, 3 * steps // 8, backward, 0)
    for h in range(heads):
        share_totals(1, h)
    lax.fori_loop(3 * steps // 8, 6 * steps // 8, backward, 0)
    for h in range(heads):
        hand_back(1, h)
    lax.fori_loop(6 * steps // 8, steps, backward, 0)

    for c in range(chunks):
        if c == chunks - 1:
            for scan in range(2):
                for h in range(heads):
                    wait_sent(scan, h)
            stat_wait(stat_send)
        for i in range(2):
            wait_near(recv_sem, 1, 1, 2 * c + i)
        for b in range(blocks):
            place_states(1, c, b, b == blocks - 1)
            if c < chunks - 1:
                row = slice(b * BLK, (b + 1) * BLK)
                last_products(
                    row, cols(c), pair[1, c, b], v, k, gk_part, gv_part, gk, gv
                )
            else:
                later[b] = pair[1, c, b]


def finish(
    normed,
    gq,
    gk_done,
    gv_done,
    gk_part,
    gv_part,
    k,
    v,
    later,
    normed_hbm,
    gq_hbm,
    gk_hbm,
    gv_hbm,
    gk,
    gv,
    out_sem,
):
    rows, columns = k.shape
    blocks = rows // BLK
    done = slice(0, columns - 2 * HD)
    rest = slice(columns - 2 * HD, columns)
    outs = []

    def write(src, dst):
        outs.append(pltpu.make_async_copy(src, dst, out_sem.at[len(outs)]))
        outs[-1].start()

    write(normed, normed_hbm)
    write(gq, gq_hbm)
    write(gk_done.at[:, done], gk_hbm.at[:, done])
    write(gv_done.at[:, done], gv_hbm.at[:, done])
    for b in range(blocks):
        row = slice(b * BLK, (b + 1) * BLK)
        last_products(row, rest, later[b], v, k, gk_part, gv_part, gk, gv)
        write(gk.at[row, rest], gk_hbm.at[row, rest])
        write(gv.at[row, rest], gv_hbm.at[row, rest])
    for copy in outs:
        copy.wait()


def shards(queries, keys, values, gain, grad_out):
    rows, columns = queries.shape
    heads = columns // HD
    chunks = heads // 2
    blocks = rows // BLK
    n_seq, n_head = lax.axis_size("seq"), lax.axis_size("head")
    out = jax.ShapeDtypeStruct((rows, columns), BF16)
    anywhere = pl.BlockSpec(memory_space=pl.ANY)
    big = pltpu.VMEM((rows, columns), BF16)
    wide = pltpu.VMEM((rows, columns), F32)
    pieces = pltpu.VMEM((2, heads, GROUP, SLICE, HD), F32)
    flops = heads * blocks * (12 * BLK * BLK * HD + 12 * BLK * HD * HD)
    vmem = pl.BlockSpec(memory_space=pltpu.VMEM)
    hbm = [
        pltpu.with_memory_space_constraint(x, pltpu.HBM)
        for x in (queries, keys, values, gain.reshape(1, columns), grad_out)
    ]
    kept = (
        pltpu.VMEM((rows, columns), BF16),
        pltpu.VMEM((rows, columns), BF16),
        pltpu.VMEM((rows, columns), BF16),
        pltpu.VMEM((rows, columns), BF16),
        pltpu.VMEM((rows, columns), F32),
        pltpu.VMEM((rows, columns), F32),
        pltpu.VMEM((rows, columns), BF16),
        pltpu.VMEM((rows, columns), BF16),
        pltpu.VMEM((blocks, 2 * HD, 2 * HD), BF16),
    )
    held = pl.pallas_call(
        functools.partial(kernel, n_seq, n_head, columns * n_head),
        out_shape=kept,
        in_specs=[anywhere] * 5,
        out_specs=(vmem,) * len(kept),
        scratch_shapes=[
            big,
            big,
            pltpu.VMEM((1, columns), F32),
            wide,
            pltpu.VMEM((columns, rows), BF16),
            wide,
            big,
            pltpu.VMEM((2, heads, HD, HD), F32),
            pieces,
            pltpu.VMEM((heads, blocks, HD, HD), BF16),
            pltpu.VMEM((2, chunks, blocks, 2 * HD, 2 * HD), BF16),
            pltpu.VMEM((heads, blocks, BLK, BLK), BF16),
            pieces,
            pieces,
            pieces,
            pltpu.VMEM((2, heads, SLICE, HD), F32),
            pltpu.VMEM((2, heads, n_seq // GROUP, SLICE, HD), F32),
            pltpu.VMEM((2 * blocks, BLK), F32),
            pltpu.VMEM((n_head, 2 * blocks, BLK), F32),
            pltpu.SemaphoreType.DMA((2 * chunks + 3,)),
            pltpu.SemaphoreType.DMA((4 * heads,)),
            pltpu.SemaphoreType.DMA((4 * heads,)),
            pltpu.SemaphoreType.DMA((2 * heads * (n_seq // GROUP - 1),)),
            pltpu.SemaphoreType.DMA((2 * heads * (n_seq // GROUP),)),
            pltpu.SemaphoreType.REGULAR,
            pltpu.SemaphoreType.DMA,
            pltpu.SemaphoreType.DMA,
        ],
        compiler_params=pltpu.CompilerParams(
            collective_id=0, has_side_effects=True, vmem_limit_bytes=32 << 20
        ),
        cost_estimate=pl.CostEstimate(
            flops=flops, bytes_accessed=4 * rows * columns * 2, transcendentals=0
        ),
    )(*hbm)
    return pl.pallas_call(
        finish,
        out_shape=(out, out, out, out),
        in_specs=[vmem] * len(kept),
        out_specs=(anywhere,) * 4,
        scratch_shapes=[big, big, pltpu.SemaphoreType.DMA((4 + 2 * blocks,))],
        compiler_params=pltpu.CompilerParams(vmem_limit_bytes=24 << 20),
        cost_estimate=pl.CostEstimate(
            flops=heads * blocks * 4 * BLK * HD * HD,
            bytes_accessed=4 * rows * columns * 2,
            transcendentals=0,
        ),
    )(*held)


def solution(mesh):
    spec = P("seq", "head")
    return jax.shard_map(
        shards,
        mesh=mesh,
        in_specs=(spec, spec, spec, P("head"), spec),
        out_specs=(spec, spec, spec, spec),
        check_vma=False,
    )
```
